128 devices in a mesh: row: 8 (over x_lo, z), col: 8 (over y, x_hi), head: 2 (over core).
Axes of the slice: x: 4 (x_hi: 2, x_lo: 2; x = x_hi * 2 + x_lo), y: 4, z: 4, core: 2. Of those that a mesh axis runs over, the one named last changes fastest.
Arguments:
- query_vectors: bfloat16 [8192, 768], P(('row', 'col'), 'head'), may hold values from -4.5 to 4.5
- key_vectors: bfloat16 [8192, 768], P(('row', 'col'), 'head'), may hold values from -4.5 to 4.5
- value_vectors: bfloat16 [8192, 768], P(('row', 'col'), 'head'), may hold values from -6 to 6
- segment_ids: int32 [8192], P(('row', 'col')), may hold values from 0 to 7, never falling along the last dimension, each value on 1 to 5120 neighbouring positions
- out_weight: bfloat16 [768, 1536], P('head'), may hold values from -0.21875 to 0.21875
- grad_output: bfloat16 [8192, 1536], P(('row', 'col')), may hold values from -6 to 6
Outputs:
- mixed_output: bfloat16 [8192, 1536], P(('row', 'col'))
- grad_queries: bfloat16 [8192, 768], P(('row', 'col'), 'head')
- grad_keys: bfloat16 [8192, 768], P(('row', 'col'), 'head')
- grad_values: bfloat16 [8192, 768], P(('row', 'col'), 'head')
The draws below stay inside these ranges and needn't reach their ends.
Inputs may be any that keep to these rules, and one draw needn't show every extreme that they name: `segment_ids`: nondecreasing along the tokens; each of the 8 images holds 1 to 5120 tokens, and one holds exactly 5120.
All inputs are finite; a program needn't handle non-finite values.
Results may differ from the reference program's by a relative error of at most 0.019.
Values may be sent and summed in bfloat16 or wider, within the bound.
No kernel may reach another device: no remote copies, remote signals or barrier semaphores. Data moves between devices by JAX's collectives and lax.ppermute only.
A program may use at most 128 MiB of HBM per device.

```python
import math
import jax
import jax.numpy as jnp
import numpy as np
from jax import lax

WIDTH = 1536
HEADS = 6
HD = 128
SEGS = 8
HW = 768
TOKENS = 8192
SEG_MOST = 5120


def draw_query_vectors(key, part):
    key = jax.random.fold_in(key, 11)
    field = jnp.clip(1.5 * jax.random.normal(key, (TOKENS, HEADS * HD), jnp.float32), -4.5, 4.5)
    return field.astype(jnp.bfloat16)


def draw_key_vectors(key, part):
    key = jax.random.fold_in(key, 12)
    field = jnp.clip(1.5 * jax.random.normal(key, (TOKENS, HEADS * HD), jnp.float32), -4.5, 4.5)
    return field.astype(jnp.bfloat16)


def level_of(stream_key, dims, pieces, least, high):
    def one(position, parts):
        heights = jax.random.uniform(jax.random.fold_in(jax.random.fold_in(stream_key, 6), position), (parts,), jnp.float32, least / len(pieces), high / len(pieces))
        return jnp.repeat(jnp.exp(heights), dims[position] // parts).reshape((-1,) + (1,) * (len(dims) - position - 1))

    factor_of = one(*pieces[0])
    for cut in pieces[1:]:
        factor_of = factor_of * one(*cut)
    return factor_of


def split_up(number_of, total, bound, slope):
    weights = [(1 << 20) // math.isqrt(grade ** slope) + 1 for grade in range(2, number_of + 1)]
    rest, given = total - bound - (number_of - 1), [1] * (number_of - 1)
    while rest > 0:
        free = [i for i in range(number_of - 1) if given[i] < bound]
        whole, budget = sum([weights[i] for i in free]), rest
        for i in free:
            more = min(bound - given[i], max(1, budget * weights[i] // whole), rest)
            given[i] = given[i] + more
            rest = rest - more
    return np.array([bound] + given)


def ragged_sizes(own_key, number_of, total, limit, skew):
    if number_of == 2:
        one = jax.random.randint(own_key, (), max(1, total - limit), min(limit, total - 1) + 1)
        return jnp.stack([one, total - one])
    tallies = jnp.asarray(split_up(number_of, total, limit, skew), jnp.int32)
    twos = (number_of - 1) // 2
    giver, taker = tallies[1:1 + 2 * twos:2], tallies[2:2 + 2 * twos:2]
    slack = jnp.minimum(giver - 1, limit - taker)
    passed = jax.random.randint(jax.random.fold_in(own_key, 1), (twos,), 0, 1 << 20) % (slack + 1)
    tallies = tallies.at[1:1 + 2 * twos:2].set(giver - passed).at[2:2 + 2 * twos:2].set(taker + passed)
    return tallies[jax.random.permutation(jax.random.fold_in(own_key, 2), number_of)]


def scatter_about(key, dims, scale, reach, split=(), held_as=jnp.bfloat16):
    values = scale * jax.random.normal(key, dims, jnp.float32)
    if split:
        values = values * level_of(key, dims, split, -0.22, 0.18)
    return jnp.clip(values, -reach, reach).astype(held_as)


def setup_inputs(seed: int = 0) -> dict:
    key_of = jax.random.split(jax.random.key(seed), 7)
    query_vectors = draw_query_vectors(jax.random.fold_in(key_of[6], 71), 0)
    key_vectors = draw_key_vectors(jax.random.fold_in(key_of[6], 71), 0)
    value_vectors = scatter_about(key_of[2], (TOKENS, HW), 1.0, 6.0, ((0, 64), (1, 2)))
    segment_ids = jnp.searchsorted(jnp.cumsum(ragged_sizes(key_of[3], SEGS, TOKENS, SEG_MOST, 1)), jnp.arange(TOKENS), side="right").astype(jnp.int32)
    out_weight = scatter_about(key_of[4], (HW, WIDTH), HW ** -0.5, 0.21875, ((0, 2),))
    grad_output = scatter_about(key_of[5], (TOKENS, WIDTH), 1.0, 6.0, ((0, 64),))
    return dict(query_vectors=query_vectors, key_vectors=key_vectors, value_vectors=value_vectors, segment_ids=segment_ids, out_weight=out_weight, grad_output=grad_output)


def masked_scores(query_block, key_block, seg_query, seg_key):
    raw_scores = jnp.dot(query_block, key_block.T, preferred_element_type=jnp.float32) * (1.0 / math.sqrt(HD))
    allowed = seg_query[:, None] == seg_key[None, :]
    return (jnp.where(allowed, raw_scores, -1e+30), allowed)

def reference(query_vectors, key_vectors, value_vectors, segment_ids, out_weight, grad_output):
    scale_factor = 1.0 / math.sqrt(HD)
    block_size = math.gcd(512, TOKENS)
    block_count = TOKENS // block_size
    grad_attn = jnp.dot(grad_output, out_weight.T, preferred_element_type=jnp.float32).astype(jnp.bfloat16)
    attn_cols, query_cols, key_cols, value_cols = ([], [], [], [])
    for head_index in range(HEADS):
        first = head_index * HD
        q_head = query_vectors[:, first:first + HD]
        k_head = key_vectors[:, first:first + HD]
        v_head = value_vectors[:, first:first + HD]
        g_head = grad_attn[:, first:first + HD]

        def query_block(block_index):
            begin = (block_index * block_size).astype(jnp.int32)
            q_block = lax.dynamic_slice_in_dim(q_head, begin, block_size, 0)
            g_block = lax.dynamic_slice_in_dim(g_head, begin, block_size, 0)
            s_block = lax.dynamic_slice_in_dim(segment_ids, begin, block_size, 0)
            scores, allowed = masked_scores(q_block, k_head, s_block, segment_ids)
            row_max = lax.optimization_barrier(jnp.max(scores, axis=1, keepdims=True))
            row_sum = lax.optimization_barrier(jnp.sum(jnp.where(allowed, jnp.exp(scores - row_max), 0.0), axis=1, keepdims=True))
            log_norm = row_max + jnp.log(row_sum)
            probs = jnp.where(allowed, jnp.exp(scores - log_norm), 0.0)
            weights = probs.astype(jnp.bfloat16)
            attn = jnp.dot(weights, v_head, preferred_element_type=jnp.float32).astype(jnp.bfloat16)
            row_delta = lax.optimization_barrier(jnp.sum(g_block.astype(jnp.float32) * attn.astype(jnp.float32), axis=1, keepdims=True))
            grad_prob = jnp.dot(g_block, v_head.T, preferred_element_type=jnp.float32)
            mix_weight = (probs * grad_prob).astype(jnp.bfloat16)
            part_mixed = jnp.dot(mix_weight, k_head, preferred_element_type=jnp.float32)
            part_plain = jnp.dot(weights, k_head, preferred_element_type=jnp.float32)
            query_grad = ((part_mixed - row_delta * part_plain) * scale_factor).astype(jnp.bfloat16)
            return (attn, log_norm[:, 0], row_delta[:, 0], query_grad)
        attn_blocks, norm_blocks, delta_blocks, grad_blocks = lax.map(query_block, jnp.arange(block_count, dtype=jnp.int32))
        attn_head = attn_blocks.reshape(TOKENS, HD)
        norm_head = norm_blocks.reshape(TOKENS)
        delta_head = delta_blocks.reshape(TOKENS)

        def key_block(block_index):
            begin = (block_index * block_size).astype(jnp.int32)
            k_block = lax.dynamic_slice_in_dim(k_head, begin, block_size, 0)
            v_block = lax.dynamic_slice_in_dim(v_head, begin, block_size, 0)
            s_block = lax.dynamic_slice_in_dim(segment_ids, begin, block_size, 0)
            scores, allowed = masked_scores(q_head, k_block, segment_ids, s_block)
            probs = jnp.where(allowed, jnp.exp(scores - norm_head[:, None]), 0.0)
            weights = probs.astype(jnp.bfloat16)
            grad_prob = jnp.dot(g_head, v_block.T, preferred_element_type=jnp.float32)
            grad_scores = (probs * (grad_prob - delta_head[:, None]) * scale_factor).astype(jnp.bfloat16)
            key_grad = jnp.dot(grad_scores.T, q_head, preferred_element_type=jnp.float32).astype(jnp.bfloat16)
            value_grad = jnp.dot(weights.T, g_head, preferred_element_type=jnp.float32).astype(jnp.bfloat16)
            return (key_grad, value_grad)
        key_blocks, value_blocks = lax.map(key_block, jnp.arange(block_count, dtype=jnp.int32))
        attn_cols.append(attn_head)
        query_cols.append(grad_blocks.reshape(TOKENS, HD))
        key_cols.append(key_blocks.reshape(TOKENS, HD))
        value_cols.append(value_blocks.reshape(TOKENS, HD))
    attn_all = jnp.concatenate(attn_cols, axis=1)
    mixed_output = jnp.dot(attn_all, out_weight, preferred_element_type=jnp.float32).astype(jnp.bfloat16)
    return (mixed_output, jnp.concatenate(query_cols, axis=1), jnp.concatenate(key_cols, axis=1), jnp.concatenate(value_cols, axis=1))
```

```python
import functools
import math

import jax
import jax.numpy as jnp
from jax import lax
from jax.experimental import pallas as pl
from jax.experimental.pallas import tpu as pltpu
from jax.sharding import PartitionSpec as P

HD = 128
TB = 128
HP = 3
PR = 2 * HP * TB
SR = 16
SCALE = 1.0 / math.sqrt(HD)
C2 = SCALE * math.log2(math.e)
FAR = 128.0
SEGS = 8
VMEM_BYTES = 48 * 1024 * 1024
F32 = jnp.float32
BF16 = jnp.bfloat16


def params():
    return pltpu.CompilerParams(vmem_limit_bytes=VMEM_BYTES)


def dot_nn(a, b):
    return lax.dot_general(a, b, (((1,), (0,)), ((), ())), preferred_element_type=F32)


def dot_nt(a, b):
    return lax.dot_general(a, b, (((1,), (1,)), ((), ())), preferred_element_type=F32)


def pack_kernel(copies, first_ref, second_ref, seg_ref, out_ref):
    seg = jnp.broadcast_to(seg_ref[...].astype(F32), (SR, TB)).astype(BF16)
    for b in range(copies):
        for h in range(HP):
            cols = slice(h * HD, (h + 1) * HD)
            out_ref[b, h * TB : (h + 1) * TB, :] = first_ref[:, cols]
            out_ref[b, (HP + h) * TB : (HP + h + 1) * TB, :] = second_ref[:, cols]
        out_ref[b, PR : PR + SR, :] = seg


def pack_grad_kernel(copies, query_ref, grad_ref, weight_ref, seg_ref, out_ref):
    seg = jnp.broadcast_to(seg_ref[...].astype(F32), (SR, TB)).astype(BF16)
    g = dot_nt(grad_ref[...], weight_ref[...]).astype(BF16)
    for b in range(copies):
        for h in range(HP):
            cols = slice(h * HD, (h + 1) * HD)
            out_ref[b, h * TB : (h + 1) * TB, :] = query_ref[:, cols]
            out_ref[b, (HP + h) * TB : (HP + h + 1) * TB, :] = g[:, cols]
        out_ref[b, PR : PR + SR, :] = seg


def pack(copies, first, second, seg):
    return pl.pallas_call(
        functools.partial(pack_kernel, copies),
        out_shape=jax.ShapeDtypeStruct((copies, PR + SR, HD), BF16),
        compiler_params=params(),
        name="pack_kv",
    )(first, second, seg)


def pack_grad(copies, query, grad_output, weight, seg):
    return pl.pallas_call(
        functools.partial(pack_grad_kernel, copies),
        out_shape=jax.ShapeDtypeStruct((copies, PR + SR, HD), BF16),
        compiler_params=params(),
        name="pack_qg",
    )(query, grad_output, weight, seg)


def fill_marks(part_ref, mark_ref, for_keys):
    for b in range(part_ref.shape[0]):
        seg = part_ref[b, PR : PR + SR, :][0:1].astype(F32)
        place = lax.broadcasted_iota(jnp.int32, (TB, TB), 0).astype(F32)
        if for_keys:
            marks = jnp.where((place != seg) & (place < SEGS), -FAR, 0.0)
        else:
            marks = jnp.where(place == seg, FAR, 0.0)
        mark_ref[b * TB : (b + 1) * TB, :] = jnp.transpose(marks).astype(BF16)


def head_rows(ref, slot):
    blocks = ref.shape[0]
    return ref[:, slot * TB : (slot + 1) * TB, :].reshape(blocks * TB, HD)


def forward_kernel(qg_ref, kv_ref, out_ref, plain_ref, mixed_ref, stat_ref, qmark, kmark, cols):
    blocks = qg_ref.shape[0]
    fill_marks(qg_ref, qmark, False)
    fill_marks(kv_ref, kmark, True)
    step = 2
    rows = step * TB
    cols[...] = jnp.zeros_like(cols)
    lane = lax.broadcasted_iota(jnp.int32, (rows, HD), 1)
    for h in range(HP):
        k = head_rows(kv_ref, h)
        v = head_rows(kv_ref, HP + h)
        k_marked = jnp.concatenate([k, kmark[...]], axis=1)
        vk = jnp.concatenate([v, k], axis=1)

        @pl.loop(0, blocks // step)
        def _(i):
            here = pl.ds(pl.multiple_of(i * rows, rows), rows)
            q = qg_ref[pl.ds(i * step, step), h * TB : (h + 1) * TB, :].reshape(rows, HD)
            g = qg_ref[pl.ds(i * step, step), (HP + h) * TB : (HP + h + 1) * TB, :].reshape(rows, HD)
            scores = dot_nt(jnp.concatenate([q, qmark[here, :]], axis=1), k_marked)
            top = jnp.max(scores, axis=1, keepdims=True)
            e = jnp.exp2((scores - top) * C2)
            total = jnp.sum(e, axis=1, keepdims=True)
            mix = e * dot_nt(g, v)
            delta = jnp.sum(mix, axis=1, keepdims=True)
            both = dot_nn(e.astype(BF16), vk)
            mixed = dot_nn(mix.astype(BF16), k)
            inv = 1.0 / total
            out_ref[h, here, :] = both[:, :HD] * inv
            plain_ref[h, here, :] = both[:, HD:] * inv
            mixed_ref[h, here, :] = mixed * inv
            norm = top * C2 + jnp.log2(total)
            cols[here, :] += jnp.where(lane == 2 * h, norm, 0.0) + jnp.where(
                lane == 2 * h + 1, delta * inv, 0.0
            )

    stat_ref[...] = jnp.transpose(cols[...])[:8, :]


def forward(qg, kv):
    n = qg.shape[0] * TB
    part = jax.ShapeDtypeStruct((HP, n, HD), F32)
    return pl.pallas_call(
        forward_kernel,
        out_shape=(part, part, part, jax.ShapeDtypeStruct((8, n), F32)),
        scratch_shapes=[
            pltpu.VMEM((n, HD), BF16),
            pltpu.VMEM((kv.shape[0] * TB, HD), BF16),
            pltpu.VMEM((n, HD), F32),
        ],
        compiler_params=params(),
        name="forward_tile",
    )(qg, kv)


def combine_kernel(all_ref, own_ref, out_ref, plain_ref, mixed_ref, send_ref, stat_ref):
    parts = all_ref.shape[0]
    n = own_ref.shape[1]
    blocks = n // TB
    stat_ref[...] = jnp.zeros_like(stat_ref)
    rows = []
    for h in range(HP):
        norms = [all_ref[c, 2 * h : 2 * h + 1, :] for c in range(parts)]
        top = functools.reduce(jnp.maximum, norms)
        norm = top + jnp.log2(sum(jnp.exp2(x - top) for x in norms))
        delta = sum(
            jnp.exp2(x - norm) * all_ref[c, 2 * h + 1 : 2 * h + 2, :] for c, x in enumerate(norms)
        )
        stat_ref[2 * h : 2 * h + 1, :] = norm
        stat_ref[2 * h + 1 : 2 * h + 2, :] = delta
        rows.append(jnp.exp2(own_ref[2 * h : 2 * h + 1, :] - norm))
        rows.append(delta)
    rows.append(jnp.zeros((TB - 2 * HP, n), F32))
    cols = jnp.transpose(jnp.concatenate(rows, axis=0))
    for h in range(HP):
        share = cols[:, 2 * h : 2 * h + 1]
        delta = cols[:, 2 * h + 1 : 2 * h + 2]
        attn = (share * out_ref[h]).astype(BF16)
        grad = (share * SCALE * (mixed_ref[h] - delta * plain_ref[h])).astype(BF16)
        send_ref[:, h * TB : (h + 1) * TB, :] = attn.reshape(blocks, TB, HD)
        send_ref[:, (HP + h) * TB : (HP + h + 1) * TB, :] = grad.reshape(blocks, TB, HD)


def combine(all_stats, own, out, plain, mixed):
    n = own.shape[1]
    return pl.pallas_call(
        combine_kernel,
        out_shape=(
            jax.ShapeDtypeStruct((n // TB, PR, HD), BF16),
            jax.ShapeDtypeStruct((8, n), F32),
        ),
        compiler_params=params(),
        name="combine_rows",
    )(all_stats, own, out, plain, mixed)


def backward_kernel(qg_ref, kv_ref, stat_ref, send_ref, qmark, kmark):
    blocks = kv_ref.shape[0]
    fill_marks(qg_ref, qmark, False)
    fill_marks(kv_ref, kmark, True)
    step = 2
    rows = step * TB
    for h in range(HP):
        q = head_rows(qg_ref, h)
        g = head_rows(qg_ref, HP + h)
        q_marked = jnp.concatenate([q, qmark[...]], axis=1)
        norm = stat_ref[2 * h : 2 * h + 1, :]
        delta = stat_ref[2 * h + 1 : 2 * h + 2, :]

        @pl.loop(0, blocks // step)
        def _(i):
            here = pl.ds(pl.multiple_of(i * rows, rows), rows)
            these = pl.ds(i * step, step)
            k = kv_ref[these, h * TB : (h + 1) * TB, :].reshape(rows, HD)
            v = kv_ref[these, (HP + h) * TB : (HP + h + 1) * TB, :].reshape(rows, HD)
            scores = dot_nt(jnp.concatenate([k, kmark[here, :]], axis=1), q_marked)
            probs = jnp.exp2(scores * C2 - norm)
            change = probs * (dot_nt(v, g) - delta)
            grad_k = dot_nn(change.astype(BF16), q) * SCALE
            grad_v = dot_nn(probs.astype(BF16), g)
            send_ref[these, h * TB : (h + 1) * TB, :] = grad_k.astype(BF16).reshape(step, TB, HD)
            send_ref[these, (HP + h) * TB : (HP + h + 1) * TB, :] = grad_v.astype(BF16).reshape(
                step, TB, HD
            )


def backward(qg, kv, stats):
    blocks = kv.shape[0]
    return pl.pallas_call(
        backward_kernel,
        out_shape=jax.ShapeDtypeStruct((blocks, PR, HD), BF16),
        scratch_shapes=[
            pltpu.VMEM((qg.shape[0] * TB, HD), BF16),
            pltpu.VMEM((blocks * TB, HD), BF16),
        ],
        compiler_params=params(),
        name="backward_tile",
    )(qg, kv, stats)


def sum_kernel(parts_ref, first_ref, second_ref):
    total = parts_ref[0].astype(F32)
    for b in range(1, parts_ref.shape[0]):
        total = total + parts_ref[b].astype(F32)
    total = total.astype(BF16)
    for h in range(HP):
        cols = slice(h * HD, (h + 1) * HD)
        first_ref[:, cols] = total[h * TB : (h + 1) * TB, :]
        second_ref[:, cols] = total[(HP + h) * TB : (HP + h + 1) * TB, :]


def sum_parts(parts, name):
    out = jax.ShapeDtypeStruct((TB, HP * HD), BF16)
    return pl.pallas_call(
        sum_kernel, out_shape=(out, out), compiler_params=params(), name=name
    )(parts)


def project_kernel(own_ref, other_ref, own_weight, other_weight, out_ref):
    out_ref[...] = (
        dot_nn(own_ref[...], own_weight[...]) + dot_nn(other_ref[...], other_weight[...])
    ).astype(BF16)


def project(own, other, own_weight, other_weight):
    return pl.pallas_call(
        project_kernel,
        out_shape=jax.ShapeDtypeStruct((TB, own_weight.shape[1]), BF16),
        compiler_params=params(),
        name="project",
    )(own, other, own_weight, other_weight)


def on_device(n_row, n_col, query, key, value, segment_ids, out_weight, grad_output):
    swap = [(0, 1), (1, 0)]
    seg = segment_ids.reshape(1, TB)
    kv = lax.all_to_all(pack(n_row, key, value, seg), "row", 0, 0)
    other_weight = lax.ppermute(out_weight, "head", swap)
    qg = lax.all_to_all(pack_grad(n_col, query, grad_output, out_weight, seg), "col", 0, 0)
    out, plain, mixed, own = forward(qg, kv)
    all_stats = lax.all_to_all(
        jnp.broadcast_to(own[None], (n_col,) + own.shape), "col", 0, 0
    )
    row_parts, stats = combine(all_stats, own, out, plain, mixed)
    row_parts = lax.all_to_all(row_parts, "col", 0, 0)
    key_parts = lax.all_to_all(backward(qg, kv, stats), "row", 0, 0)
    attn, grad_queries = sum_parts(row_parts, "sum_rows")
    other_attn = lax.ppermute(attn, "head", swap)
    mixed_output = project(attn, other_attn, out_weight, other_weight)
    grad_keys, grad_values = sum_parts(key_parts, "sum_keys")
    return (mixed_output, grad_queries, grad_keys, grad_values)


def solution(mesh):
    tokens = P(("row", "col"))
    heads = P(("row", "col"), "head")
    whole = P(("row", "col"), None)
    return jax.shard_map(
        functools.partial(on_device, mesh.shape["row"], mesh.shape["col"]),
        mesh=mesh,
        in_specs=(heads, heads, heads, tokens, P("head", None), whole),
        out_specs=(whole, heads, heads, heads),
        check_vma=False,
    )
```

```python
import functools
import math

import jax
import jax.numpy as jnp
from jax import lax
from jax.experimental import pallas as pl
from jax.experimental.pallas import tpu as pltpu
from jax.sharding import PartitionSpec as P

HD = 128
TB = 128
HP = 3
PR = 2 * HP * TB
SR = 16
SCALE = 1.0 / math.sqrt(HD)
C2 = SCALE * math.log2(math.e)
FAR = 128.0
SEGS = 8
VMEM_BYTES = 12 * 1024 * 1024
ALL_VMEM = 63_000_000
F32 = jnp.float32
BF16 = jnp.bfloat16
WHOLE = pl.BlockSpec(memory_space=pltpu.VMEM)
ANYWHERE = pl.BlockSpec(memory_space=pl.ANY)


def call(
    kernel, name, out_shape, args, scratch=(), anywhere=0, vmem=VMEM_BYTES, flops=0, moved=0, exps=0
):
    return pl.pallas_call(
        kernel,
        out_shape=out_shape,
        in_specs=[ANYWHERE] * anywhere + [WHOLE] * (len(args) - anywhere),
        out_specs=jax.tree.map(lambda _: WHOLE, out_shape),
        scratch_shapes=list(scratch),
        compiler_params=pltpu.CompilerParams(vmem_limit_bytes=vmem),
        cost_estimate=pl.CostEstimate(flops=flops, bytes_accessed=moved, transcendentals=exps),
        name=name,
    )(*args)


def shape(dims, dtype):
    return jax.ShapeDtypeStruct(dims, dtype)


def dot_nn(a, b):
    return lax.dot_general(a, b, (((1,), (0,)), ((), ())), preferred_element_type=F32)


def dot_nt(a, b):
    return lax.dot_general(a, b, (((1,), (1,)), ((), ())), preferred_element_type=F32)


def write_block(first, second, seg_ref, out_ref):
    for h in range(HP):
        cols = slice(h * HD, (h + 1) * HD)
        out_ref[h * TB : (h + 1) * TB, :] = first[:, cols]
        out_ref[(HP + h) * TB : (HP + h + 1) * TB, :] = second[:, cols]
    out_ref[PR : PR + SR, :] = jnp.broadcast_to(seg_ref[...].astype(F32), (SR, TB)).astype(BF16)


def fetch(sources, held, sems):
    copies = [pltpu.make_async_copy(a, b, sems.at[i]) for i, (a, b) in enumerate(zip(sources, held))]
    for copy in copies:
        copy.start()
    for copy in copies:
        copy.wait()


def pack_kernel(*refs):
    sources, (out_ref, *held, sems) = refs[1:4], refs[4:]
    fetch(sources, held, sems)
    seg, first, second = held
    write_block(first[...], second[...], seg, out_ref)


def pack_grad_kernel(*refs):
    sources, (out_ref, *held, sems) = refs[:4], refs[4:]
    fetch(sources, held, sems)
    seg, query, grad, weight = held
    write_block(query[...], dot_nt(grad[...], weight[...]).astype(BF16), seg, out_ref)


def pack(kernel, name, later, *args):
    block = shape((PR + SR, HD), BF16)
    scratch = [pltpu.VMEM(a.shape, a.dtype) for a in args] + [pltpu.SemaphoreType.DMA((len(args),))]
    args = later + args
    return call(kernel, name, block, args, scratch, len(args), ALL_VMEM, moved=2**22)


def stack_kernel(*refs):
    *sources, out_ref, sems = refs
    sources = sources[-out_ref.shape[0] :]
    fetch(sources, [out_ref.at[i] for i in range(len(sources))], sems)


def stack(name, blocks, later=()):
    out = shape((len(blocks),) + blocks[0].shape, BF16)
    return pl.pallas_call(
        stack_kernel,
        out_shape=out,
        in_specs=[ANYWHERE] * (len(later) + len(blocks)),
        out_specs=ANYWHERE,
        scratch_shapes=[pltpu.SemaphoreType.DMA((len(blocks),))],
        compiler_params=pltpu.CompilerParams(vmem_limit_bytes=VMEM_BYTES),
        cost_estimate=pl.CostEstimate(flops=0, bytes_accessed=2 * out.size * 2, transcendentals=0),
        name=name,
    )(*later, *blocks)


def fill_marks(part_refs, mark_ref, for_keys):
    place = lax.broadcasted_iota(jnp.int32, (TB, TB), 0).astype(F32)
    start = 0
    for part_ref in part_refs:
        for b in range(part_ref.shape[0]):
            seg = part_ref[b, PR : PR + SR, :][0:1].astype(F32)
            if for_keys:
                marks = jnp.where((place != seg) & (place < SEGS), -FAR, 0.0)
            else:
                marks = jnp.where(place == seg, FAR, 0.0)
            mark_ref[start : start + TB, :] = jnp.transpose(marks).astype(BF16)
            start += TB


def head_rows(refs, slot):
    return jnp.concatenate(
        [
            ref[:, slot * TB : (slot + 1) * TB, :].reshape(ref.shape[0] * TB, HD)
            for ref in refs
        ],
        axis=0,
    )


STEP = 2
ROWS = STEP * TB


def merge(first, second):
    top = jnp.maximum(first[0], second[0])
    norm = top + jnp.log2(jnp.exp2(first[0] - top) + jnp.exp2(second[0] - top))
    delta = jnp.exp2(first[0] - norm) * first[1] + jnp.exp2(second[0] - norm) * second[1]
    return norm, delta


def chunk_rows(ref, slot):
    return ref[:, slot * TB : (slot + 1) * TB, :].reshape(ROWS, HD)


def stats_kernel(count, first, *refs):
    chunks, (ko_ref, kx_ref), refs = refs[:count], refs[count : count + 2], refs[count + 2 :]
    kmark, (cols_ref, rows_ref, qmark) = (refs[3], refs[:3]) if first else (refs[0], refs[1:])
    if first:
        fill_marks((ko_ref, kx_ref), kmark, True)
    fill_marks(chunks, qmark, False)
    cols_ref[...] = jnp.zeros_like(cols_ref)
    lane = lax.broadcasted_iota(jnp.int32, (ROWS, HD), 1)
    for h in range(HP):
        k = jnp.concatenate([head_rows((ko_ref, kx_ref), h), kmark[...]], axis=1)
        v = head_rows((ko_ref, kx_ref), HP + h)
        for i, chunk in enumerate(chunks):
            here = slice(i * ROWS, (i + 1) * ROWS)
            q, g = chunk_rows(chunk, h), chunk_rows(chunk, HP + h)
            scores = dot_nt(jnp.concatenate([q, qmark[here, :]], axis=1), k)
            top = jnp.max(scores, axis=1, keepdims=True)
            e = jnp.exp2((scores - top) * C2)
            total = jnp.sum(e, axis=1, keepdims=True)
            delta = jnp.sum(e * dot_nt(g, v), axis=1, keepdims=True) / total
            norm = top * C2 + jnp.log2(total)
            cols_ref[here, :] += jnp.where(lane == 2 * h, norm, 0.0) + jnp.where(
                lane == 2 * h + 1, delta, 0.0
            )
    rows_ref[...] = jnp.transpose(cols_ref[...])[:8, :]


def stats(name, chunks, ko, kx, kmark=None):
    n, m = len(chunks) * ROWS, 2 * ko.shape[0] * TB
    out = (shape((n, HD), F32), shape((8, n), F32), shape((n, HD), BF16))
    args = tuple(chunks) + (ko, kx)
    if kmark is None:
        out += (shape((m, HD), BF16),)
    else:
        args += (kmark,)
    return call(
        functools.partial(stats_kernel, len(chunks), kmark is None), name, out, args,
        flops=12 * n * m * HP * HD, moved=2**22, exps=n * m * HP,
    )


def forward_kernel(count, *refs):
    chunks, (ko_ref, kx_ref, kmark), refs = refs[:count], refs[count : count + 3], refs[count + 3 :]
    qmarks, cols, out_ref = refs[:count], refs[count : 2 * count], refs[-1]
    for h in range(HP):
        k = head_rows((ko_ref, kx_ref), h)
        v = head_rows((ko_ref, kx_ref), HP + h)
        k_marked = jnp.concatenate([k, kmark[...]], axis=1)
        vk = jnp.concatenate([v, k], axis=1)
        for i, (chunk, (qmark, at), (norm, _)) in enumerate(zip(chunks, qmarks, cols)):
            here, there = slice(i * ROWS, (i + 1) * ROWS), slice(at, at + ROWS)
            q, g = chunk_rows(chunk, h), chunk_rows(chunk, HP + h)
            scores = dot_nt(jnp.concatenate([q, qmark[there, :]], axis=1), k_marked)
            p = jnp.exp2(scores * C2 - norm[there, 2 * h : 2 * h + 1])
            mix = p * dot_nt(g, v)
            out_ref[h, here, : 2 * HD] = dot_nn(p.astype(BF16), vk)
            out_ref[h, here, 2 * HD :] = dot_nn(mix.astype(BF16), k)


def forward(name, chunks, ko, kx, kmark, qmarks, cols):
    n, m = len(chunks) * ROWS, 2 * ko.shape[0] * TB
    starts = [at for _, at in qmarks]

    def kernel(*refs):
        fixed = len(chunks) + 3
        marks = list(zip(refs[fixed : fixed + len(chunks)], starts))
        norms = list(zip(refs[fixed + len(chunks) : -1], starts))
        forward_kernel(len(chunks), *refs[:fixed], *marks, *norms, refs[-1])

    args = tuple(chunks) + (ko, kx, kmark) + tuple(a for a, _ in qmarks) + tuple(a for a, _ in cols)
    return call(
        kernel, name, shape((HP, n, 3 * HD), F32), args,
        flops=12 * n * m * 2 * HD * HP, moved=8 * 2**20, exps=n * m * HP,
    )


def pair_kernel(later_ref, *refs):
    del later_ref
    mine_ref, got_ref, out_ref = refs
    out_ref[...] = jnp.zeros_like(out_ref)
    for block in range(mine_ref.shape[1] // TB):
        mine = slice(block * TB, (block + 1) * TB)
        theirs = slice((block ^ 1) * TB, ((block ^ 1) + 1) * TB)
        for r in range(0, 2 * HP, 2):
            norm, delta = merge(
                (mine_ref[r : r + 1, mine], mine_ref[r + 1 : r + 2, mine]),
                (got_ref[r : r + 1, theirs], got_ref[r + 1 : r + 2, theirs]),
            )
            out_ref[r : r + 1, mine] = norm
            out_ref[r + 1 : r + 2, mine] = delta


def pair(later, mine, got):
    return call(pair_kernel, "pair_rows", shape(mine.shape, F32), (later, mine, got), anywhere=1)


def combine_kernel(steps, *refs):
    chunks = len(steps)
    members, refs = refs[:chunks], refs[chunks:]
    rows_ref, outs, sends, stat_ref = refs[0], refs[1:3], refs[3:-1], refs[-1]
    stat_ref[...] = jnp.zeros_like(stat_ref)
    for i, mine in enumerate(steps):
        here = slice(i * ROWS, (i + 1) * ROWS)
        found = []
        for member, step in zip(members, steps):
            at = steps.index((mine - step) % chunks) * ROWS
            found.append(member[:, at : at + ROWS])
        for r in range(0, 2 * HP, 2):
            norm, delta = functools.reduce(merge, [(f[r : r + 1], f[r + 1 : r + 2]) for f in found])
            stat_ref[r : r + 1, here] = norm
            stat_ref[r + 1 : r + 2, here] = delta
    rows = []
    for r in range(0, 2 * HP, 2):
        rows.append(jnp.exp2(rows_ref[r : r + 1, :] - stat_ref[r : r + 1, :]))
        rows.append(stat_ref[r + 1 : r + 2, :])
    rows.append(jnp.zeros((TB - 2 * HP, chunks * ROWS), F32))
    cols = jnp.transpose(jnp.concatenate(rows, axis=0))
    for i, send_ref in enumerate(sends):
        here = slice(i * ROWS, (i + 1) * ROWS)
        out_ref, start = outs[i // (chunks // 2)], i % (chunks // 2) * ROWS
        there = slice(start, start + ROWS)
        for h in range(HP):
            share = cols[here, 2 * h : 2 * h + 1]
            delta = cols[here, 2 * h + 1 : 2 * h + 2]
            attn, plain, mixed = (out_ref[h, there, c * HD : (c + 1) * HD] for c in range(3))
            attn = (share * attn).astype(BF16)
            grad = (share * SCALE * (mixed - delta * plain)).astype(BF16)
            send_ref[:, h * TB : (h + 1) * TB, :] = attn.reshape(STEP, TB, HD)
            send_ref[:, (HP + h) * TB : (HP + h + 1) * TB, :] = grad.reshape(STEP, TB, HD)


def combine(steps, *args):
    rows = args[0].shape[1]
    send = shape((STEP, PR, HD), BF16)
    return call(
        functools.partial(combine_kernel, steps), "combine_rows",
        (send,) * len(steps) + (shape((8, rows), F32),), args,
        flops=5 * rows * HD * HP * 2, moved=6 * 2**20,
    )


def backward_kernel(count, first, k_ref, *refs):
    chunks, (kmark, *qmarks, stat_ref, send_ref) = refs[:count], refs[count:]
    marks = jnp.concatenate([m[...] for m in qmarks], axis=0)
    for h in range(HP):
        q = head_rows(chunks, h)
        g = head_rows(chunks, HP + h)
        q_marked = jnp.concatenate([q, marks], axis=1)
        norm, delta = (stat_ref[r : r + 1, :] for r in (2 * h, 2 * h + 1))

        for i in range(k_ref.shape[0] // STEP):
            here = slice(first * TB + i * ROWS, first * TB + (i + 1) * ROWS)
            these = slice(i * STEP, (i + 1) * STEP)
            k, v = (
                k_ref[these, slot * TB : (slot + 1) * TB, :].reshape(ROWS, HD)
                for slot in (h, HP + h)
            )
            scores = dot_nt(jnp.concatenate([k, kmark[here, :]], axis=1), q_marked)
            probs = jnp.exp2(scores * C2 - norm)
            change = probs * (dot_nt(v, g) - delta)
            grad_k = (dot_nn(change.astype(BF16), q) * SCALE).astype(BF16)
            grad_v = dot_nn(probs.astype(BF16), g).astype(BF16)
            send_ref[these, h * TB : (h + 1) * TB, :] = grad_k.reshape(STEP, TB, HD)
            send_ref[these, (HP + h) * TB : (HP + h + 1) * TB, :] = grad_v.reshape(STEP, TB, HD)


def backward(name, first, k, chunks, kmark, qmarks, stat):
    n, m = len(chunks) * ROWS, k.shape[0] * TB
    args = (k, *chunks, kmark, *qmarks, stat)
    return call(
        functools.partial(backward_kernel, len(chunks), first), name,
        shape((k.shape[0], PR, HD), BF16), args,
        flops=10 * n * m * 2 * HD * HP, moved=8 * 2**20, exps=n * m * HP,
    )


def partner_sum_kernel(later_ref, *refs):
    del later_ref
    *parts, all_ref, attn_ref, own_ref = refs
    total = sum(ref[1].astype(F32) for ref in parts).astype(BF16)
    all_ref[...] = total
    attn_ref[...] = total[: PR // 2]
    own_ref[...] = sum(ref[0, : PR // 2, :].astype(F32) for ref in parts).astype(BF16)


def partner_sum(parts, later):
    out = (shape((PR, HD), BF16), shape((PR // 2, HD), BF16), shape((PR // 2, HD), BF16))
    return call(
        partner_sum_kernel, "sum_partner", out, (later, *parts), anywhere=1,
        moved=len(parts) * PR * HD * 2,
    )


def add_kernel(later_ref, own_ref, got_ref, *out_refs):
    del later_ref
    for j, out_ref in enumerate(out_refs):
        out_ref[...] = (own_ref[j].astype(F32) + got_ref[j].astype(F32)).astype(BF16)


def add(own, got, name, later):
    out = tuple(shape(own.shape[1:], BF16) for _ in range(own.shape[0]))
    args = (later, own, got)
    return call(add_kernel, name, out, args, anywhere=1, flops=own.size, moved=6 * own.size)


def sum_kernel(*refs):
    parts, (first_ref, second_ref) = refs[:-2], refs[-2:]
    parts = [part[0] if len(part.shape) == 3 else part[...] for part in parts]
    total = sum(part.astype(F32) for part in parts).astype(BF16)
    for h in range(HP):
        cols = slice(h * HD, (h + 1) * HD)
        first_ref[:, cols] = total[h * TB : (h + 1) * TB, :]
        second_ref[:, cols] = total[(HP + h) * TB : (HP + h + 1) * TB, :]


def sum_parts(parts, name):
    out = shape((TB, HP * HD), BF16)
    size = sum(p.size for p in parts)
    return call(sum_kernel, name, (out, out), tuple(parts), flops=size, moved=2 * size)


def finish_kernel(*refs):
    *parts, got, other_own, other_got, weight, other_weight, out_ref, query_ref = refs
    total = sum(part[0].astype(F32) for part in parts) + got[...].astype(F32)
    total = total.astype(BF16)
    other = (other_own[...].astype(F32) + other_got[...].astype(F32)).astype(BF16)
    for h in range(HP):
        query_ref[:, h * HD : (h + 1) * HD] = total[(HP + h) * TB : (HP + h + 1) * TB, :]
    attn, other = (
        jnp.concatenate([rows[h * TB : (h + 1) * TB, :] for h in range(HP)], axis=1)
        for rows in (total, other)
    )
    out_ref[...] = (dot_nn(attn, weight[...]) + dot_nn(other, other_weight[...])).astype(BF16)


def finish(parts, got, other_own, other_got, weight, other_weight):
    out = (shape((TB, weight.shape[1]), BF16), shape((TB, HP * HD), BF16))
    args = (*parts, got, other_own, other_got, weight, other_weight)
    return call(
        finish_kernel, "finish_rows", out, args,
        flops=4 * TB * weight.size, moved=4 * weight.size,
    )


class Places:
    def __init__(self, n_row, n_col):
        self.n_row, self.n_col = n_row, n_col
        self.ny, self.nz = n_col // 2, n_row // 2

    def of(self, index):
        row, col = divmod(index, self.n_col)
        low, z = divmod(row, self.nz)
        y, high = divmod(col, 2)
        return high, low, y, z

    def index(self, high, low, y, z):
        return (low * self.nz + z) * self.n_col + y * 2 + high

    def send(self, array, move, turn=0):
        pairs = []
        for i in range(self.n_row * self.n_col):
            for core in range(2):
                target = self.index(*move(core, *self.of(i)))
                pairs.append((2 * i + core, 2 * target + (core ^ turn)))
        return lax.ppermute(array, ("row", "col", "head"), pairs)

    def along_y(self, array, by):
        return self.send(array, lambda core, high, low, y, z: (high, low, (y + by) % self.ny, z))

    def along_z(self, array, by):
        return self.send(array, lambda core, high, low, y, z: (high, low, y, (z + by) % self.nz))

    def query_partner(self, array):
        return self.send(array, lambda core, high, low, y, z: (high ^ 1 ^ core, low ^ 1, y, z))

    def query_partner_other_core(self, array):
        return self.send(
            array, lambda core, high, low, y, z: (high ^ 1 ^ core, low ^ 1, y, z), 1
        )

    def key_partner(self, array):
        return self.send(array, lambda core, high, low, y, z: (high ^ core, low ^ 1, y, z))


def shifts(n):
    return [0] + sorted(range(1, n), key=lambda d: min(d, n - d))


def on_device(places, query, key, value, segment_ids, out_weight, grad_output):
    swap = [(0, 1), (1, 0)]
    y_shifts, z_shifts = shifts(places.ny), shifts(places.nz)
    seg = segment_ids.reshape(1, TB)

    qg = pack(pack_grad_kernel, "pack_qg", (), seg, query, grad_output, out_weight)
    kv = pack(pack_kernel, "pack_kv", (qg,), seg, key, value)
    pair0 = stack("stack_qg", [qg, places.query_partner(qg)])
    chunks = [pair0] + [places.along_y(pair0, d) for d in y_shifts[1:]]
    ko = stack("stack_kv", [kv] + [places.along_z(kv, d) for d in z_shifts[1:]], (pair0,))
    kx = places.key_partner(ko)
    other_weight = lax.ppermute(out_weight, "head", swap)

    count = len(chunks)
    parts, marked = [], []
    kmark = None
    for name, some in (("first", range(0, 1)), ("near", range(1, count - 1)), ("last", [count - 1])):
        if len(some) == 0:
            continue
        cols, rows, qmark, *made = stats("stats_" + name, [chunks[i] for i in some], ko, kx, kmark)
        kmark = made[0] if made else kmark
        parts.append(rows)
        marked.append(qmark)
        if name == "first":
            where = []
        where += [((qmark, j * ROWS), (cols, j * ROWS)) for j in range(len(some))]
    rows = jnp.concatenate(parts, axis=1)
    got = places.query_partner(rows)
    outs = []
    for name, some in (
        ("forward_near", range(count // 2)), ("forward_far", range(count // 2, count))
    ):
        if outs:
            pair_rows = pair(outs[0], rows, got)
            all_rows = [pair_rows] + [places.along_y(pair_rows, d) for d in y_shifts[1:]]
        outs.append(
            forward(
                name, [chunks[i] for i in some], ko, kx, kmark,
                [where[i][0] for i in some], [where[i][1] for i in some],
            )
        )
    *sends, stat = combine(y_shifts, *all_rows, rows, *outs)

    row_parts = [sends[0]] + [
        places.along_y(part, -d) for part, d in zip(sends[1:], y_shifts[1:])
    ]
    key_partner = backward("backward_partner", places.nz, kx, chunks, kmark, marked, stat)
    key_got = places.key_partner(key_partner)
    key_own = backward("backward_own", 0, ko, chunks, kmark, marked, stat)

    key_parts = add(key_own, key_got, "add_keys", stat)
    key_parts = [key_parts[0]] + [
        places.along_z(part, -d) for part, d in zip(key_parts[1:], z_shifts[1:])
    ]
    partner_rows, partner_attn, own_attn = partner_sum(row_parts, key_parts[0])
    mixed_output, grad_queries = finish(
        row_parts,
        places.query_partner(partner_rows),
        lax.ppermute(own_attn, "head", swap),
        places.query_partner_other_core(partner_attn),
        out_weight,
        other_weight,
    )
    grad_keys, grad_values = sum_parts(key_parts, "sum_keys")
    return (mixed_output, grad_queries, grad_keys, grad_values)


def solution(mesh):
    tokens = P(("row", "col"))
    heads = P(("row", "col"), "head")
    whole = P(("row", "col"), None)
    places = Places(mesh.shape["row"], mesh.shape["col"])
    return jax.shard_map(
        functools.partial(on_device, places),
        mesh=mesh,
        in_specs=(heads, heads, heads, tokens, P("head", None), whole),
        out_specs=(whole, heads, heads, heads),
        check_vma=False,
    )
```

```python
import functools
import math

import jax
import jax.numpy as jnp
from jax import lax
from jax.experimental import pallas as pl
from jax.experimental.pallas import tpu as pltpu
from jax.sharding import PartitionSpec as P

HD = 128
TB = 128
HP = 3
PR = 2 * HP * TB
SR = 16
SCALE = 1.0 / math.sqrt(HD)
C2 = SCALE * math.log2(math.e)
FAR = 128.0
SEGS = 8
VMEM_BYTES = 12 * 1024 * 1024
ALL_VMEM = 63_000_000
F32 = jnp.float32
BF16 = jnp.bfloat16
WHOLE = pl.BlockSpec(memory_space=pltpu.VMEM)
ANYWHERE = pl.BlockSpec(memory_space=pl.ANY)


def call(
    kernel, name, out_shape, args, scratch=(), anywhere=0, vmem=VMEM_BYTES, flops=0, moved=0, exps=0
):
    return pl.pallas_call(
        kernel,
        out_shape=out_shape,
        in_specs=[ANYWHERE] * anywhere + [WHOLE] * (len(args) - anywhere),
        out_specs=jax.tree.map(lambda _: WHOLE, out_shape),
        scratch_shapes=list(scratch),
        compiler_params=pltpu.CompilerParams(vmem_limit_bytes=vmem),
        cost_estimate=pl.CostEstimate(flops=flops, bytes_accessed=moved, transcendentals=exps),
        name=name,
    )(*args)


def shape(dims, dtype):
    return jax.ShapeDtypeStruct(dims, dtype)


def dot_nn(a, b):
    return lax.dot_general(a, b, (((1,), (0,)), ((), ())), preferred_element_type=F32)


def dot_nt(a, b):
    return lax.dot_general(a, b, (((1,), (1,)), ((), ())), preferred_element_type=F32)


def write_block(first, second, seg_ref, out_ref):
    for h in range(HP):
        cols = slice(h * HD, (h + 1) * HD)
        out_ref[h * TB : (h + 1) * TB, :] = first[:, cols]
        out_ref[(HP + h) * TB : (HP + h + 1) * TB, :] = second[:, cols]
    out_ref[PR : PR + SR, :] = jnp.broadcast_to(seg_ref[...].astype(F32), (SR, TB)).astype(BF16)


def fetch(sources, held, sems):
    copies = [pltpu.make_async_copy(a, b, sems.at[i]) for i, (a, b) in enumerate(zip(sources, held))]
    for copy in copies:
        copy.start()
    for copy in copies:
        copy.wait()


def pack_kernel(*refs):
    sources, (kv_ref, qg_ref), (*held, sems) = refs[:6], refs[6:8], refs[8:]
    fetch(sources, held, sems)
    seg, key, value, query, grad, weight = held
    write_block(key[...], value[...], seg, kv_ref)
    write_block(query[...], dot_nt(grad[...], weight[...]).astype(BF16), seg, qg_ref)


def pack(*args):
    block = shape((PR + SR, HD), BF16)
    scratch = [pltpu.VMEM(a.shape, a.dtype) for a in args] + [pltpu.SemaphoreType.DMA((len(args),))]
    return call(pack_kernel, "pack", (block, block), args, scratch, len(args), ALL_VMEM)


def gate_kernel(source_ref, *refs):
    del source_ref, refs


def gate(array, *later):
    return pl.pallas_call(
        gate_kernel,
        out_shape=shape(array.shape, array.dtype),
        in_specs=[ANYWHERE] * (1 + len(later)),
        out_specs=ANYWHERE,
        input_output_aliases={0: 0},
        cost_estimate=pl.CostEstimate(flops=0, bytes_accessed=0, transcendentals=0),
        name="gate",
    )(array, *later)


def fill_marks(part_refs, mark_ref, for_keys):
    place = lax.broadcasted_iota(jnp.int32, (TB, TB), 0).astype(F32)
    start = 0
    for part_ref in part_refs:
        for b in range(part_ref.shape[0]):
            seg = part_ref[b, PR : PR + SR, :][0:1].astype(F32)
            if for_keys:
                marks = jnp.where((place != seg) & (place < SEGS), -FAR, 0.0)
            else:
                marks = jnp.where(place == seg, FAR, 0.0)
            mark_ref[start : start + TB, :] = jnp.transpose(marks).astype(BF16)
            start += TB


def head_rows(refs, slot):
    return jnp.concatenate(
        [
            ref[:, slot * TB : (slot + 1) * TB, :].reshape(ref.shape[0] * TB, HD)
            for ref in refs
        ],
        axis=0,
    )


STEP = 2
ROWS = STEP * TB


def merge(first, second):
    top = jnp.maximum(first[0], second[0])
    norm = top + jnp.log2(jnp.exp2(first[0] - top) + jnp.exp2(second[0] - top))
    delta = jnp.exp2(first[0] - norm) * first[1] + jnp.exp2(second[0] - norm) * second[1]
    return norm, delta


def chunk_rows(ref, slot):
    return ref[:, slot * TB : (slot + 1) * TB, :].reshape(ROWS, HD)


def stats_part(tasks, qmark, cols_ref, rows_ref):
    cols_ref[...] = jnp.zeros_like(cols_ref)
    for h in range(HP):
        for key_refs, kmarks, chunks in tasks:
            marks = jnp.concatenate([m[...] for m in kmarks], axis=0)
            k = jnp.concatenate([head_rows(key_refs, h), marks], axis=1)
            v = head_rows(key_refs, HP + h)
            for chunk, i in chunks:
                here = slice(i * ROWS, (i + 1) * ROWS)
                q, g = chunk_rows(chunk, h), chunk_rows(chunk, HP + h)
                scores = dot_nt(jnp.concatenate([q, qmark[here, :]], axis=1), k)
                top = jnp.max(scores, axis=1, keepdims=True)
                e = jnp.exp2((scores - top) * C2)
                cols_ref[here, 3 * h : 3 * h + 1] = top
                cols_ref[here, 3 * h + 1 : 3 * h + 2] = jnp.sum(e, axis=1, keepdims=True)
                cols_ref[here, 3 * h + 2 : 3 * h + 3] = jnp.sum(
                    e * dot_nt(g, v), axis=1, keepdims=True
                )
    found = jnp.transpose(cols_ref[...])
    rows_ref[...] = jnp.zeros_like(rows_ref)
    for h in range(HP):
        top, total, delta = (found[r : r + 1, :] for r in range(3 * h, 3 * h + 3))
        rows_ref[2 * h : 2 * h + 1, :] = top * C2 + jnp.log2(total)
        rows_ref[2 * h + 1 : 2 * h + 2, :] = delta / total


def early_stats_kernel(*refs):
    *chunks, key_ref, rows_ref, qmark, kmark, cols_ref = refs
    fill_marks(chunks, qmark, False)
    fill_marks((key_ref,), kmark, True)
    chunks = [(chunk, i) for i, chunk in enumerate(chunks)]
    stats_part([((key_ref,), (kmark,), chunks)], qmark, cols_ref, rows_ref)


def all_stats_kernel(early, count, *refs):
    chunks, refs = refs[:count], refs[count:]
    ko_ref, kx_ref, kmark_o, early_mark, before_ref, cols_ref, rows_ref, qmark, kmark_x = refs
    fill_marks((kx_ref,), kmark_x, True)
    late = [i for i in range(count) if i not in early]
    for j, i in enumerate(early):
        qmark[i * ROWS : (i + 1) * ROWS, :] = early_mark[j * ROWS : (j + 1) * ROWS, :]
    for i in late:
        fill_marks((chunks[i],), qmark.at[i * ROWS : (i + 1) * ROWS, :], False)
    tasks = [
        ((kx_ref,), (kmark_x,), [(chunks[i], i) for i in early]),
        ((ko_ref, kx_ref), (kmark_o, kmark_x), [(chunks[i], i) for i in late]),
    ]
    stats_part(tasks, qmark, cols_ref, rows_ref)
    for j, i in enumerate(early):
        then, here = slice(j * ROWS, (j + 1) * ROWS), slice(i * ROWS, (i + 1) * ROWS)
        for r in range(0, 2 * HP, 2):
            norm, delta = merge(
                (before_ref[r : r + 1, then], before_ref[r + 1 : r + 2, then]),
                (rows_ref[r : r + 1, here], rows_ref[r + 1 : r + 2, here]),
            )
            rows_ref[r : r + 1, here] = norm
            rows_ref[r + 1 : r + 2, here] = delta
    rows = rows_ref[...]
    rest = jnp.zeros((HD - rows.shape[0], rows.shape[1]), F32)
    cols_ref[...] = jnp.transpose(jnp.concatenate([rows, rest], axis=0))


def early_stats(chunks, key):
    n, m = len(chunks) * ROWS, key.shape[0] * TB
    out = (shape((8, n), F32), shape((n, HD), BF16), shape((m, HD), BF16))
    scratch = [pltpu.VMEM((n, HD), F32)]
    return call(early_stats_kernel, "stats_early", out, (*chunks, key), scratch)


def all_stats(early, chunks, *args):
    n, m = len(chunks) * ROWS, args[1].shape[0] * TB
    out = (shape((n, HD), F32), shape((8, n), F32), shape((n, HD), BF16), shape((m, HD), BF16))
    kernel = functools.partial(all_stats_kernel, early, len(chunks))
    return call(kernel, "stats_all", out, (*chunks, *args))


def forward_kernel(first, *refs):
    *chunks, ko_ref, kx_ref, kmark_o, kmark_x, qmark, norm_ref, out_ref = refs
    marks = jnp.concatenate([kmark_o[...], kmark_x[...]], axis=0)
    for h in range(HP):
        k = head_rows((ko_ref, kx_ref), h)
        v = head_rows((ko_ref, kx_ref), HP + h)
        k_marked = jnp.concatenate([k, marks], axis=1)
        vk = jnp.concatenate([v, k], axis=1)
        for i, chunk in enumerate(chunks):
            here = slice(i * ROWS, (i + 1) * ROWS)
            there = slice((first + i) * ROWS, (first + i + 1) * ROWS)
            q, g = chunk_rows(chunk, h), chunk_rows(chunk, HP + h)
            scores = dot_nt(jnp.concatenate([q, qmark[there, :]], axis=1), k_marked)
            p = jnp.exp2(scores * C2 - norm_ref[there, 2 * h : 2 * h + 1])
            mix = p * dot_nt(g, v)
            out_ref[h, here, : 2 * HD] = dot_nn(p.astype(BF16), vk)
            out_ref[h, here, 2 * HD :] = dot_nn(mix.astype(BF16), k)


def forward(name, first, chunks, *args):
    n, m = len(chunks) * ROWS, 2 * args[0].shape[0] * TB
    return call(
        functools.partial(forward_kernel, first), name, shape((HP, n, 3 * HD), F32),
        (*chunks, *args), flops=12 * n * m * 2 * HD * HP, moved=8 * 2**20, exps=n * m * HP,
    )


def pair_kernel(later_ref, *refs):
    del later_ref
    mine_ref, got_ref, out_ref = refs
    out_ref[...] = jnp.zeros_like(out_ref)
    for block in range(mine_ref.shape[1] // TB):
        mine = slice(block * TB, (block + 1) * TB)
        theirs = slice((block ^ 1) * TB, ((block ^ 1) + 1) * TB)
        for r in range(0, 2 * HP, 2):
            norm, delta = merge(
                (mine_ref[r : r + 1, mine], mine_ref[r + 1 : r + 2, mine]),
                (got_ref[r : r + 1, theirs], got_ref[r + 1 : r + 2, theirs]),
            )
            out_ref[r : r + 1, mine] = norm
            out_ref[r + 1 : r + 2, mine] = delta


def pair(later, mine, got):
    return call(pair_kernel, "pair_rows", shape(mine.shape, F32), (later, mine, got), anywhere=1)


def whole_kernel(steps, later_ref, *refs):
    del later_ref
    *members, stat_ref = refs
    stat_ref[...] = jnp.zeros_like(stat_ref)
    for i, mine in enumerate(steps):
        here = slice(i * ROWS, (i + 1) * ROWS)
        found = []
        for member, step in zip(members, steps):
            at = steps.index((mine - step) % len(steps)) * ROWS
            found.append(member[:, at : at + ROWS])
        for r in range(0, 2 * HP, 2):
            norm, delta = functools.reduce(merge, [(f[r : r + 1], f[r + 1 : r + 2]) for f in found])
            stat_ref[r : r + 1, here] = norm
            stat_ref[r + 1 : r + 2, here] = delta


def whole(steps, members, later):
    out = shape(members[0].shape, F32)
    return call(functools.partial(whole_kernel, steps), "whole_rows", out, (later, *members), anywhere=1)


def share_kernel(chunks, later_ref, stat_ref, rows_ref, *refs):
    del later_ref
    outs, sends, partners = refs[:2], refs[2 : 2 + chunks], refs[2 + chunks :]
    partners = [None] * (chunks - len(partners)) + list(partners)
    rows = []
    for r in range(0, 2 * HP, 2):
        rows.append(jnp.exp2(rows_ref[r : r + 1, :] - stat_ref[r : r + 1, :]))
        rows.append(stat_ref[r + 1 : r + 2, :])
    rows.append(jnp.zeros((TB - 2 * HP, chunks * ROWS), F32))
    cols = jnp.transpose(jnp.concatenate(rows, axis=0))
    for i, send_ref in enumerate(sends):
        here = slice(i * ROWS, (i + 1) * ROWS)
        out_ref, start = outs[i // (chunks // 2)], i % (chunks // 2) * ROWS
        there = slice(start, start + ROWS)
        for h in range(HP):
            share = cols[here, 2 * h : 2 * h + 1]
            delta = cols[here, 2 * h + 1 : 2 * h + 2]
            attn, plain, mixed = (out_ref[h, there, c * HD : (c + 1) * HD] for c in range(3))
            attn = (share * attn).astype(BF16)
            grad = (share * SCALE * (mixed - delta * plain)).astype(BF16)
            for slot, value in ((h, attn), (HP + h, grad)):
                there_rows = slice(slot * TB, (slot + 1) * TB)
                send_ref[0, there_rows, :] = value[:TB]
                if partners[i] is None:
                    send_ref[1, there_rows, :] = value[TB:]
                else:
                    partners[i][there_rows, :] = value[TB:]


def shares(chunks, far, later, *args):
    out = (shape((STEP, PR, HD), BF16),) * (chunks - far) + (shape((1, PR, HD), BF16),) * far
    out += (shape((PR, HD), BF16),) * far
    return call(
        functools.partial(share_kernel, chunks), "share_rows", out, (later, *args), anywhere=1,
        moved=4 * 2**20,
    )


def backward_kernel(count, k_ref, *refs):
    chunks, (kmark, qmark, stat_ref, send_ref) = refs[:count], refs[count:]
    marks = qmark[...]
    for h in range(HP):
        q = head_rows(chunks, h)
        g = head_rows(chunks, HP + h)
        q_marked = jnp.concatenate([q, marks], axis=1)
        norm, delta = (stat_ref[r : r + 1, :] for r in (2 * h, 2 * h + 1))

        for i in range(k_ref.shape[0] // STEP):
            here = slice(i * ROWS, (i + 1) * ROWS)
            these = slice(i * STEP, (i + 1) * STEP)
            k, v = (
                k_ref[these, slot * TB : (slot + 1) * TB, :].reshape(ROWS, HD)
                for slot in (h, HP + h)
            )
            scores = dot_nt(jnp.concatenate([k, kmark[here, :]], axis=1), q_marked)
            probs = jnp.exp2(scores * C2 - norm)
            change = probs * (dot_nt(v, g) - delta)
            grad_k = (dot_nn(change.astype(BF16), q) * SCALE).astype(BF16)
            grad_v = dot_nn(probs.astype(BF16), g).astype(BF16)
            send_ref[these, h * TB : (h + 1) * TB, :] = grad_k.reshape(STEP, TB, HD)
            send_ref[these, (HP + h) * TB : (HP + h + 1) * TB, :] = grad_v.reshape(STEP, TB, HD)


def backward(name, k, chunks, kmark, qmark, stat):
    n, m = len(chunks) * ROWS, k.shape[0] * TB
    args = (k, *chunks, kmark, qmark, stat)
    return call(
        functools.partial(backward_kernel, len(chunks)), name,
        shape((k.shape[0], PR, HD), BF16), args,
        flops=10 * n * m * 2 * HD * HP, moved=8 * 2**20, exps=n * m * HP,
    )


def partner_sum_kernel(later_ref, *refs):
    del later_ref
    refs[-1][...] = sum(ref[1].astype(F32) for ref in refs[:-1]).astype(BF16)


def partner_sum(parts, later):
    return call(
        partner_sum_kernel, "sum_partner", shape((PR, HD), BF16), (later, *parts), anywhere=1,
        moved=len(parts) * PR * HD * 2,
    )


def far_sum_kernel(later_ref, mine_ref, got_ref, out_ref):
    del later_ref
    out_ref[...] = (mine_ref[0].astype(F32) + got_ref[...].astype(F32)).astype(BF16)


def far_sum(mine, got, later):
    args = (later, mine, got)
    return call(far_sum_kernel, "sum_far", shape((PR, HD), BF16), args, anywhere=1)


def add_kernel(later_ref, own_ref, got_ref, *out_refs):
    del later_ref
    for j, out_ref in enumerate(out_refs):
        out_ref[...] = (own_ref[j].astype(F32) + got_ref[j].astype(F32)).astype(BF16)


def add(own, got, name, later):
    out = tuple(shape(own.shape[1:], BF16) for _ in range(own.shape[0]))
    args = (later, own, got)
    return call(add_kernel, name, out, args, anywhere=1, flops=own.size, moved=6 * own.size)


def sum_kernel(skip, *refs):
    parts, (first_ref, second_ref) = refs[skip:-2], refs[-2:]
    parts = [part[0] if len(part.shape) == 3 else part[...] for part in parts]
    total = sum(part.astype(F32) for part in parts).astype(BF16)
    for h in range(HP):
        cols = slice(h * HD, (h + 1) * HD)
        first_ref[:, cols] = total[h * TB : (h + 1) * TB, :]
        second_ref[:, cols] = total[(HP + h) * TB : (HP + h + 1) * TB, :]


def sum_parts(parts, name, later=()):
    out = shape((TB, HP * HD), BF16)
    size = sum(p.size for p in parts)
    kernel, args = functools.partial(sum_kernel, len(later)), (*later, *parts)
    return call(kernel, name, (out, out), args, anywhere=len(later), flops=size, moved=2 * size)


def project_kernel(own_ref, other_ref, own_weight, other_weight, out_ref, token_ref):
    token_ref[...] = jnp.zeros_like(token_ref)
    out_ref[...] = (
        dot_nn(own_ref[...], own_weight[...]) + dot_nn(other_ref[...], other_weight[...])
    ).astype(BF16)


def project(own, other, own_weight, other_weight):
    width = own_weight.shape[1]
    return call(
        project_kernel, "project", (shape((TB, width), BF16), shape((8, HD), F32)),
        (own, other, own_weight, other_weight),
        flops=4 * own.size * width, moved=4 * own_weight.size,
    )


class Places:
    def __init__(self, n_row, n_col):
        self.n_row, self.n_col = n_row, n_col
        self.ny, self.nz = n_col // 2, n_row // 2

    def of(self, index):
        row, col = divmod(index, self.n_col)
        low, z = divmod(row, self.nz)
        y, high = divmod(col, 2)
        return high, low, y, z

    def index(self, high, low, y, z):
        return (low * self.nz + z) * self.n_col + y * 2 + high

    def send(self, array, move):
        pairs = []
        for i in range(self.n_row * self.n_col):
            for core in range(2):
                target = self.index(*move(core, *self.of(i)))
                pairs.append((2 * i + core, 2 * target + core))
        return lax.ppermute(array, ("row", "col", "head"), pairs)

    def along_y(self, array, by):
        return self.send(array, lambda core, high, low, y, z: (high, low, (y + by) % self.ny, z))

    def along_z(self, array, by):
        return self.send(array, lambda core, high, low, y, z: (high, low, y, (z + by) % self.nz))

    def query_partner(self, array):
        return self.send(array, lambda core, high, low, y, z: (high ^ 1 ^ core, low ^ 1, y, z))

    def query_partner_along_y(self, array, by):
        return self.send(
            array,
            lambda core, high, low, y, z: (high ^ 1 ^ core, low ^ 1, (y + by) % self.ny, z),
        )

    def key_partner(self, array):
        return self.send(array, lambda core, high, low, y, z: (high ^ core, low ^ 1, y, z))


def shifts(n):
    return [0] + sorted(range(1, n), key=lambda d: min(d, n - d))


def on_device(places, query, key, value, segment_ids, out_weight, grad_output):
    swap = [(0, 1), (1, 0)]
    y_shifts, z_shifts = shifts(places.ny), shifts(places.nz)
    seg = segment_ids.reshape(1, TB)

    kv, qg = pack(seg, key, value, query, grad_output, out_weight)
    pair0 = jnp.stack([qg, places.query_partner(qg)])
    far = [d for d in y_shifts if 1 < d == places.ny - d]
    near = [d for d in y_shifts[1:] if d not in far]
    chunks = [pair0] + [places.along_y(pair0, d) for d in near]
    far_blocks = [places.along_y(qg, d) for d in far]
    far_partner_blocks = [places.query_partner_along_y(qg, d) for d in far]
    chunks += [jnp.stack(pair) for pair in zip(far_blocks, far_partner_blocks)]
    key_blocks = [places.along_z(kv, d) for d in z_shifts[1:]]
    key_blocks[-1] = gate(key_blocks[-1], pair0, *far_blocks, *far_partner_blocks)
    ko = jnp.stack([kv] + key_blocks)
    kx = places.key_partner(ko)
    other_weight = lax.ppermute(out_weight, "head", swap)

    count = len(chunks)
    early = [i for i in range(count) if not 1 <= i <= len(near)]
    early_rows, early_mark, kmark_o = early_stats([chunks[i] for i in early], ko)
    cols, rows, qmark, kmark_x = all_stats(early, chunks, ko, kx, kmark_o, early_mark, early_rows)
    got = places.query_partner(rows)
    halves = []
    for name, first in (("forward_near", 0), ("forward_far", count // 2)):
        if halves:
            pair_rows = pair(halves[0], rows, got)
            members = [pair_rows] + [places.along_y(pair_rows, d) for d in y_shifts[1:]]
        some = chunks[first : first + count // 2]
        halves.append(forward(name, first, some, ko, kx, kmark_o, kmark_x, qmark, cols))
    stat = whole(y_shifts, members, halves[1])
    key_partner = backward("backward_partner", kx, chunks, kmark_x, qmark, stat)
    key_got = places.key_partner(key_partner)

    made = shares(count, len(far), key_partner, stat, rows, *halves)
    sends, far_partners = made[:count], made[count:]
    row_parts = [sends[0]] + [places.along_y(part, -d) for part, d in zip(sends[1:], near)]
    far_parts = sends[len(row_parts) :]
    far_got = [places.query_partner(far_rows) for far_rows in far_partners]
    key_own = backward("backward_own", ko, chunks, kmark_o, qmark, stat)
    far_parts = [
        places.along_y(far_sum(part, got, key_own), -d)
        for part, got, d in zip(far_parts, far_got, far)
    ]

    key_parts = add(key_own, key_got, "add_keys", stat)
    key_parts = [key_parts[0]] + [
        places.along_z(part, -d) for part, d in zip(key_parts[1:], z_shifts[1:])
    ]
    row_got = places.query_partner(partner_sum(row_parts, key_parts[0]))
    attn, grad_queries = sum_parts(row_parts + far_parts + [row_got], "sum_rows")
    other_attn = lax.ppermute(attn, "head", swap)
    mixed_output, token = project(attn, other_attn, out_weight, other_weight)
    grad_keys, grad_values = sum_parts(key_parts, "sum_keys", (token,))
    return (mixed_output, grad_queries, grad_keys, grad_values)


def solution(mesh):
    tokens = P(("row", "col"))
    heads = P(("row", "col"), "head")
    whole = P(("row", "col"), None)
    places = Places(mesh.shape["row"], mesh.shape["col"])
    return jax.shard_map(
        functools.partial(on_device, places),
        mesh=mesh,
        in_specs=(heads, heads, heads, tokens, P("head", None), whole),
        out_specs=(whole, heads, heads, heads),
        check_vma=False,
    )
```

```python
import functools
import math

import jax
import jax.numpy as jnp
from jax import lax
from jax.experimental import pallas as pl
from jax.experimental.pallas import tpu as pltpu
from jax.sharding import PartitionSpec as P

HD = 128
TB = 128
HP = 3
PR = 2 * HP * TB
SR = 16
SCALE = 1.0 / math.sqrt(HD)
C2 = SCALE * math.log2(math.e)
FAR = 128.0
SEGS = 8
VMEM_BYTES = 12 * 1024 * 1024
ALL_VMEM = 63_000_000
F32 = jnp.float32
BF16 = jnp.bfloat16
WHOLE = pl.BlockSpec(memory_space=pltpu.VMEM)
ANYWHERE = pl.BlockSpec(memory_space=pl.ANY)


def call(
    kernel, name, out_shape, args, scratch=(), anywhere=0, vmem=VMEM_BYTES, flops=0, moved=0, exps=0
):
    return pl.pallas_call(
        kernel,
        out_shape=out_shape,
        in_specs=[ANYWHERE] * anywhere + [WHOLE] * (len(args) - anywhere),
        out_specs=jax.tree.map(lambda _: WHOLE, out_shape),
        scratch_shapes=list(scratch),
        compiler_params=pltpu.CompilerParams(vmem_limit_bytes=vmem),
        cost_estimate=pl.CostEstimate(flops=flops, bytes_accessed=moved, transcendentals=exps),
        name=name,
    )(*args)


def shape(dims, dtype):
    return jax.ShapeDtypeStruct(dims, dtype)


def dot_nn(a, b):
    return lax.dot_general(a, b, (((1,), (0,)), ((), ())), preferred_element_type=F32)


def dot_nt(a, b):
    return lax.dot_general(a, b, (((1,), (1,)), ((), ())), preferred_element_type=F32)


def write_block(first, second, seg_ref, out_ref):
    for h in range(HP):
        cols = slice(h * HD, (h + 1) * HD)
        out_ref[h * TB : (h + 1) * TB, :] = first[:, cols]
        out_ref[(HP + h) * TB : (HP + h + 1) * TB, :] = second[:, cols]
    out_ref[PR : PR + SR, :] = jnp.broadcast_to(seg_ref[...].astype(F32), (SR, TB)).astype(BF16)


def fetch(sources, held, sems):
    copies = [pltpu.make_async_copy(a, b, sems.at[i]) for i, (a, b) in enumerate(zip(sources, held))]
    for copy in copies:
        copy.start()
    for copy in copies:
        copy.wait()


def pack_kernel(*refs):
    sources, (kv_ref, qg_ref), (*held, sems) = refs[:6], refs[6:8], refs[8:]
    fetch(sources, held, sems)
    seg, key, value, query, grad, weight = held
    write_block(key[...], value[...], seg, kv_ref)
    write_block(query[...], dot_nt(grad[...], weight[...]).astype(BF16), seg, qg_ref)


def pack(*args):
    block = shape((PR + SR, HD), BF16)
    scratch = [pltpu.VMEM(a.shape, a.dtype) for a in args] + [pltpu.SemaphoreType.DMA((len(args),))]
    return call(pack_kernel, "pack", (block, block), args, scratch, len(args), ALL_VMEM)


def fill_marks(part_refs, mark_ref, for_keys):
    place = lax.broadcasted_iota(jnp.int32, (TB, TB), 0).astype(F32)
    start = 0
    for part_ref in part_refs:
        for b in range(part_ref.shape[0]):
            seg = part_ref[b, PR : PR + SR, :][0:1].astype(F32)
            if for_keys:
                marks = jnp.where((place != seg) & (place < SEGS), -FAR, 0.0)
            else:
                marks = jnp.where(place == seg, FAR, 0.0)
            mark_ref[start : start + TB, :] = jnp.transpose(marks).astype(BF16)
            start += TB


def head_rows(refs, slot):
    return jnp.concatenate(
        [
            ref[:, slot * TB : (slot + 1) * TB, :].reshape(ref.shape[0] * TB, HD)
            for ref in refs
        ],
        axis=0,
    )


STEP = 2
ROWS = STEP * TB


def merge(first, second):
    top = jnp.maximum(first[0], second[0])
    norm = top + jnp.log2(jnp.exp2(first[0] - top) + jnp.exp2(second[0] - top))
    delta = jnp.exp2(first[0] - norm) * first[1] + jnp.exp2(second[0] - norm) * second[1]
    return norm, delta


def chunk_rows(ref, slot):
    return ref[:, slot * TB : (slot + 1) * TB, :].reshape(ROWS, HD)


def stats_part(tasks, qmark, cols_ref, rows_ref):
    cols_ref[...] = jnp.zeros_like(cols_ref)
    for h in range(HP):
        for key_refs, kmarks, chunks in tasks:
            marks = jnp.concatenate([m[...] for m in kmarks], axis=0)
            k = jnp.concatenate([head_rows(key_refs, h), marks], axis=1)
            v = head_rows(key_refs, HP + h)
            for chunk, i in chunks:
                here = slice(i * ROWS, (i + 1) * ROWS)
                q, g = chunk_rows(chunk, h), chunk_rows(chunk, HP + h)
                scores = dot_nt(jnp.concatenate([q, qmark[here, :]], axis=1), k)
                top = jnp.max(scores, axis=1, keepdims=True)
                e = jnp.exp2((scores - top) * C2)
                cols_ref[here, 3 * h : 3 * h + 1] = top
                cols_ref[here, 3 * h + 1 : 3 * h + 2] = jnp.sum(e, axis=1, keepdims=True)
                cols_ref[here, 3 * h + 2 : 3 * h + 3] = jnp.sum(
                    e * dot_nt(g, v), axis=1, keepdims=True
                )
    found = jnp.transpose(cols_ref[...])
    rows_ref[...] = jnp.zeros_like(rows_ref)
    for h in range(HP):
        top, total, delta = (found[r : r + 1, :] for r in range(3 * h, 3 * h + 3))
        rows_ref[2 * h : 2 * h + 1, :] = top * C2 + jnp.log2(total)
        rows_ref[2 * h + 1 : 2 * h + 2, :] = delta / total


def early_stats_kernel(*refs):
    *chunks, key_ref, rows_ref, qmark, kmark, cols_ref = refs
    fill_marks(chunks, qmark, False)
    fill_marks((key_ref,), kmark, True)
    chunks = [(chunk, i) for i, chunk in enumerate(chunks)]
    stats_part([((key_ref,), (kmark,), chunks)], qmark, cols_ref, rows_ref)


def all_stats_kernel(early, count, *refs):
    chunks, refs = refs[:count], refs[count:]
    ko_ref, kx_ref, kmark_o, early_mark, before_ref, cols_ref, rows_ref, qmark, kmark_x = refs
    fill_marks((kx_ref,), kmark_x, True)
    late = [i for i in range(count) if i not in early]
    for j, i in enumerate(early):
        qmark[i * ROWS : (i + 1) * ROWS, :] = early_mark[j * ROWS : (j + 1) * ROWS, :]
    for i in late:
        fill_marks((chunks[i],), qmark.at[i * ROWS : (i + 1) * ROWS, :], False)
    tasks = [
        ((kx_ref,), (kmark_x,), [(chunks[i], i) for i in early]),
        ((ko_ref, kx_ref), (kmark_o, kmark_x), [(chunks[i], i) for i in late]),
    ]
    stats_part(tasks, qmark, cols_ref, rows_ref)
    for j, i in enumerate(early):
        then, here = slice(j * ROWS, (j + 1) * ROWS), slice(i * ROWS, (i + 1) * ROWS)
        for r in range(0, 2 * HP, 2):
            norm, delta = merge(
                (before_ref[r : r + 1, then], before_ref[r + 1 : r + 2, then]),
                (rows_ref[r : r + 1, here], rows_ref[r + 1 : r + 2, here]),
            )
            rows_ref[r : r + 1, here] = norm
            rows_ref[r + 1 : r + 2, here] = delta
    rows = rows_ref[...]
    rest = jnp.zeros((HD - rows.shape[0], rows.shape[1]), F32)
    cols_ref[...] = jnp.transpose(jnp.concatenate([rows, rest], axis=0))


def early_stats(chunks, key):
    n, m = len(chunks) * ROWS, key.shape[0] * TB
    out = (shape((8, n), F32), shape((n, HD), BF16), shape((m, HD), BF16))
    scratch = [pltpu.VMEM((n, HD), F32)]
    return call(early_stats_kernel, "stats_early", out, (*chunks, key), scratch)


def all_stats(early, chunks, *args):
    n, m = len(chunks) * ROWS, args[1].shape[0] * TB
    out = (shape((n, HD), F32), shape((8, n), F32), shape((n, HD), BF16), shape((m, HD), BF16))
    kernel = functools.partial(all_stats_kernel, early, len(chunks))
    return call(kernel, "stats_all", out, (*chunks, *args))


def forward_kernel(first, *refs):
    *chunks, ko_ref, kx_ref, kmark_o, kmark_x, qmark, norm_ref, out_ref = refs
    marks = jnp.concatenate([kmark_o[...], kmark_x[...]], axis=0)
    for h in range(HP):
        k = head_rows((ko_ref, kx_ref), h)
        v = head_rows((ko_ref, kx_ref), HP + h)
        k_marked = jnp.concatenate([k, marks], axis=1)
        vk = jnp.concatenate([v, k], axis=1)
        for i, chunk in enumerate(chunks):
            here = slice(i * ROWS, (i + 1) * ROWS)
            there = slice((first + i) * ROWS, (first + i + 1) * ROWS)
            q, g = chunk_rows(chunk, h), chunk_rows(chunk, HP + h)
            scores = dot_nt(jnp.concatenate([q, qmark[there, :]], axis=1), k_marked)
            p = jnp.exp2(scores * C2 - norm_ref[there, 2 * h : 2 * h + 1])
            mix = p * dot_nt(g, v)
            out_ref[h, here, : 2 * HD] = dot_nn(p.astype(BF16), vk)
            out_ref[h, here, 2 * HD :] = dot_nn(mix.astype(BF16), k)


def forward(name, first, chunks, *args):
    n, m = len(chunks) * ROWS, 2 * args[0].shape[0] * TB
    return call(
        functools.partial(forward_kernel, first), name, shape((HP, n, 3 * HD), F32),
        (*chunks, *args), flops=12 * n * m * 2 * HD * HP, moved=8 * 2**20, exps=n * m * HP,
    )


def pair_kernel(later_ref, *refs):
    del later_ref
    mine_ref, got_ref, out_ref = refs
    out_ref[...] = jnp.zeros_like(out_ref)
    for block in range(mine_ref.shape[1] // TB):
        mine = slice(block * TB, (block + 1) * TB)
        theirs = slice((block ^ 1) * TB, ((block ^ 1) + 1) * TB)
        for r in range(0, 2 * HP, 2):
            norm, delta = merge(
                (mine_ref[r : r + 1, mine], mine_ref[r + 1 : r + 2, mine]),
                (got_ref[r : r + 1, theirs], got_ref[r + 1 : r + 2, theirs]),
            )
            out_ref[r : r + 1, mine] = norm
            out_ref[r + 1 : r + 2, mine] = delta


def pair(later, mine, got):
    return call(pair_kernel, "pair_rows", shape(mine.shape, F32), (later, mine, got), anywhere=1)


def whole_kernel(steps, later_ref, *refs):
    del later_ref
    *members, stat_ref = refs
    stat_ref[...] = jnp.zeros_like(stat_ref)
    for i, mine in enumerate(steps):
        here = slice(i * ROWS, (i + 1) * ROWS)
        found = []
        for member, step in zip(members, steps):
            at = steps.index((mine - step) % len(steps)) * ROWS
            found.append(member[:, at : at + ROWS])
        for r in range(0, 2 * HP, 2):
            norm, delta = functools.reduce(merge, [(f[r : r + 1], f[r + 1 : r + 2]) for f in found])
            stat_ref[r : r + 1, here] = norm
            stat_ref[r + 1 : r + 2, here] = delta


def whole(steps, members, later):
    out = shape(members[0].shape, F32)
    return call(functools.partial(whole_kernel, steps), "whole_rows", out, (later, *members), anywhere=1)


def share_kernel(chunks, later_ref, stat_ref, rows_ref, *refs):
    del later_ref
    outs, sends, partners = refs[:2], refs[2 : 2 + chunks], refs[2 + chunks :]
    partners = [None] * (chunks - len(partners)) + list(partners)
    rows = []
    for r in range(0, 2 * HP, 2):
        rows.append(jnp.exp2(rows_ref[r : r + 1, :] - stat_ref[r : r + 1, :]))
        rows.append(stat_ref[r + 1 : r + 2, :])
    rows.append(jnp.zeros((TB - 2 * HP, chunks * ROWS), F32))
    cols = jnp.transpose(jnp.concatenate(rows, axis=0))
    for i, send_ref in enumerate(sends):
        here = slice(i * ROWS, (i + 1) * ROWS)
        out_ref, start = outs[i // (chunks // 2)], i % (chunks // 2) * ROWS
        there = slice(start, start + ROWS)
        for h in range(HP):
            share = cols[here, 2 * h : 2 * h + 1]
            delta = cols[here, 2 * h + 1 : 2 * h + 2]
            attn, plain, mixed = (out_ref[h, there, c * HD : (c + 1) * HD] for c in range(3))
            attn = (share * attn).astype(BF16)
            grad = (share * SCALE * (mixed - delta * plain)).astype(BF16)
            for slot, value in ((h, attn), (HP + h, grad)):
                there_rows = slice(slot * TB, (slot + 1) * TB)
                send_ref[0, there_rows, :] = value[:TB]
                if partners[i] is None:
                    send_ref[1, there_rows, :] = value[TB:]
                else:
                    partners[i][there_rows, :] = value[TB:]


def shares(chunks, far, later, *args):
    out = (shape((STEP, PR, HD), BF16),) * (chunks - far) + (shape((1, PR, HD), BF16),) * far
    out += (shape((PR, HD), BF16),) * far
    return call(
        functools.partial(share_kernel, chunks), "share_rows", out, (later, *args), anywhere=1,
        moved=4 * 2**20,
    )


def backward_kernel(count, k_ref, *refs):
    chunks, (kmark, qmark, stat_ref, send_ref) = refs[:count], refs[count:]
    marks = qmark[...]
    for h in range(HP):
        q = head_rows(chunks, h)
        g = head_rows(chunks, HP + h)
        q_marked = jnp.concatenate([q, marks], axis=1)
        norm, delta = (stat_ref[r : r + 1, :] for r in (2 * h, 2 * h + 1))

        for i in range(k_ref.shape[0] // STEP):
            here = slice(i * ROWS, (i + 1) * ROWS)
            these = slice(i * STEP, (i + 1) * STEP)
            k, v = (
                k_ref[these, slot * TB : (slot + 1) * TB, :].reshape(ROWS, HD)
                for slot in (h, HP + h)
            )
            scores = dot_nt(jnp.concatenate([k, kmark[here, :]], axis=1), q_marked)
            probs = jnp.exp2(scores * C2 - norm)
            change = probs * (dot_nt(v, g) - delta)
            grad_k = (dot_nn(change.astype(BF16), q) * SCALE).astype(BF16)
            grad_v = dot_nn(probs.astype(BF16), g).astype(BF16)
            send_ref[these, h * TB : (h + 1) * TB, :] = grad_k.reshape(STEP, TB, HD)
            send_ref[these, (HP + h) * TB : (HP + h + 1) * TB, :] = grad_v.reshape(STEP, TB, HD)


def backward(name, k, chunks, kmark, qmark, stat):
    n, m = len(chunks) * ROWS, k.shape[0] * TB
    args = (k, *chunks, kmark, qmark, stat)
    return call(
        functools.partial(backward_kernel, len(chunks)), name,
        shape((k.shape[0], PR, HD), BF16), args,
        flops=10 * n * m * 2 * HD * HP, moved=8 * 2**20, exps=n * m * HP,
    )


def partner_sum_kernel(later_ref, *refs):
    del later_ref
    refs[-1][...] = sum(ref[1].astype(F32) for ref in refs[:-1]).astype(BF16)


def partner_sum(parts, later):
    return call(
        partner_sum_kernel, "sum_partner", shape((PR, HD), BF16), (later, *parts), anywhere=1,
        moved=len(parts) * PR * HD * 2,
    )


def far_sum_kernel(later_ref, mine_ref, got_ref, out_ref):
    del later_ref
    out_ref[...] = (mine_ref[0].astype(F32) + got_ref[...].astype(F32)).astype(BF16)


def far_sum(mine, got, later):
    args = (later, mine, got)
    return call(far_sum_kernel, "sum_far", shape((PR, HD), BF16), args, anywhere=1)


def add_kernel(later_ref, own_ref, got_ref, *out_refs):
    del later_ref
    for j, out_ref in enumerate(out_refs):
        out_ref[...] = (own_ref[j].astype(F32) + got_ref[j].astype(F32)).astype(BF16)


def add(own, got, name, later):
    out = tuple(shape(own.shape[1:], BF16) for _ in range(own.shape[0]))
    args = (later, own, got)
    return call(add_kernel, name, out, args, anywhere=1, flops=own.size, moved=6 * own.size)


def sum_kernel(skip, *refs):
    parts, (first_ref, second_ref) = refs[skip:-2], refs[-2:]
    parts = [part[0] if len(part.shape) == 3 else part[...] for part in parts]
    total = sum(part.astype(F32) for part in parts).astype(BF16)
    for h in range(HP):
        cols = slice(h * HD, (h + 1) * HD)
        first_ref[:, cols] = total[h * TB : (h + 1) * TB, :]
        second_ref[:, cols] = total[(HP + h) * TB : (HP + h + 1) * TB, :]


def sum_parts(parts, name, later=()):
    out = shape((TB, HP * HD), BF16)
    size = sum(p.size for p in parts)
    kernel, args = functools.partial(sum_kernel, len(later)), (*later, *parts)
    return call(kernel, name, (out, out), args, anywhere=len(later), flops=size, moved=2 * size)


def project_kernel(own_ref, other_ref, own_weight, other_weight, out_ref, token_ref):
    token_ref[...] = jnp.zeros_like(token_ref)
    out_ref[...] = (
        dot_nn(own_ref[...], own_weight[...]) + dot_nn(other_ref[...], other_weight[...])
    ).astype(BF16)


def project(own, other, own_weight, other_weight):
    width = own_weight.shape[1]
    return call(
        project_kernel, "project", (shape((TB, width), BF16), shape((8, HD), F32)),
        (own, other, own_weight, other_weight),
        flops=4 * own.size * width, moved=4 * own_weight.size,
    )


class Places:
    def __init__(self, n_row, n_col):
        self.n_row, self.n_col = n_row, n_col
        self.ny, self.nz = n_col // 2, n_row // 2

    def of(self, index):
        row, col = divmod(index, self.n_col)
        low, z = divmod(row, self.nz)
        y, high = divmod(col, 2)
        return high, low, y, z

    def index(self, high, low, y, z):
        return (low * self.nz + z) * self.n_col + y * 2 + high

    def send(self, array, move):
        pairs = []
        for i in range(self.n_row * self.n_col):
            for core in range(2):
                target = self.index(*move(core, *self.of(i)))
                pairs.append((2 * i + core, 2 * target + core))
        return lax.ppermute(array, ("row", "col", "head"), pairs)

    def along_y(self, array, by):
        return self.send(array, lambda core, high, low, y, z: (high, low, (y + by) % self.ny, z))

    def along_z(self, array, by):
        return self.send(array, lambda core, high, low, y, z: (high, low, y, (z + by) % self.nz))

    def query_partner(self, array):
        return self.send(array, lambda core, high, low, y, z: (high ^ 1 ^ core, low ^ 1, y, z))

    def query_partner_along_y(self, array, by):
        return self.send(
            array,
            lambda core, high, low, y, z: (high ^ 1 ^ core, low ^ 1, (y + by) % self.ny, z),
        )

    def key_partner(self, array):
        return self.send(array, lambda core, high, low, y, z: (high ^ core, low ^ 1, y, z))


def shifts(n):
    return [0] + sorted(range(1, n), key=lambda d: min(d, n - d))


def on_device(places, query, key, value, segment_ids, out_weight, grad_output):
    swap = [(0, 1), (1, 0)]
    y_shifts, z_shifts = shifts(places.ny), shifts(places.nz)
    seg = segment_ids.reshape(1, TB)

    kv, qg = pack(seg, key, value, query, grad_output, out_weight)
    pair0 = jnp.stack([qg, places.query_partner(qg)])
    far = [d for d in y_shifts if 1 < d == places.ny - d]
    near = [d for d in y_shifts[1:] if d not in far]
    chunks = [pair0] + [places.along_y(pair0, d) for d in near]
    far_blocks = [places.along_y(qg, d) for d in far]
    far_partner_blocks = [places.query_partner_along_y(qg, d) for d in far]
    chunks += [jnp.stack(pair) for pair in zip(far_blocks, far_partner_blocks)]
    key_blocks = [places.along_z(kv, d) for d in z_shifts[1:]]
    (kv, *key_blocks), *_ = lax.optimization_barrier(
        ((kv, *key_blocks), pair0, *far_blocks, *far_partner_blocks)
    )
    ko = jnp.stack([kv] + key_blocks)
    kx = places.key_partner(ko)
    other_weight = lax.ppermute(out_weight, "head", swap)

    count = len(chunks)
    early = [i for i in range(count) if not 1 <= i <= len(near)]
    early_rows, early_mark, kmark_o = early_stats([chunks[i] for i in early], ko)
    cols, rows, qmark, kmark_x = all_stats(early, chunks, ko, kx, kmark_o, early_mark, early_rows)
    got = places.query_partner(rows)
    halves = []
    for name, first in (("forward_near", 0), ("forward_far", count // 2)):
        if halves:
            pair_rows = pair(halves[0], rows, got)
            members = [pair_rows] + [places.along_y(pair_rows, d) for d in y_shifts[1:]]
        some = chunks[first : first + count // 2]
        halves.append(forward(name, first, some, ko, kx, kmark_o, kmark_x, qmark, cols))
    stat = whole(y_shifts, members, halves[1])
    key_partner = backward("backward_partner", kx, chunks, kmark_x, qmark, stat)
    key_got = places.key_partner(key_partner)

    made = shares(count, len(far), key_partner, stat, rows, *halves)
    sends, far_partners = made[:count], made[count:]
    row_parts = [sends[0]] + [places.along_y(part, -d) for part, d in zip(sends[1:], near)]
    far_parts = sends[len(row_parts) :]
    far_got = [places.query_partner(far_rows) for far_rows in far_partners]
    key_own = backward("backward_own", ko, chunks, kmark_o, qmark, stat)
    far_parts = [
        places.along_y(far_sum(part, got, key_own), -d)
        for part, got, d in zip(far_parts, far_got, far)
    ]

    key_parts = add(key_own, key_got, "add_keys", stat)
    key_parts = [key_parts[0]] + [
        places.along_z(part, -d) for part, d in zip(key_parts[1:], z_shifts[1:])
    ]
    row_got = places.query_partner(partner_sum(row_parts, key_parts[0]))
    attn, grad_queries = sum_parts(row_parts + far_parts + [row_got], "sum_rows")
    other_attn = lax.ppermute(attn, "head", swap)
    mixed_output, token = project(attn, other_attn, out_weight, other_weight)
    grad_keys, grad_values = sum_parts(key_parts, "sum_keys", (token,))
    return (mixed_output, grad_queries, grad_keys, grad_values)


def solution(mesh):
    tokens = P(("row", "col"))
    heads = P(("row", "col"), "head")
    whole = P(("row", "col"), None)
    places = Places(mesh.shape["row"], mesh.shape["col"])
    return jax.shard_map(
        functools.partial(on_device, places),
        mesh=mesh,
        in_specs=(heads, heads, heads, tokens, P("head", None), whole),
        out_specs=(whole, heads, heads, heads),
        check_vma=False,
    )
```

```python
import functools
import math

import jax
import jax.numpy as jnp
from jax import lax
from jax.experimental import pallas as pl
from jax.experimental.pallas import tpu as pltpu
from jax.sharding import PartitionSpec as P

HD = 128
TB = 128
HP = 3
PR = 2 * HP * TB
SR = 16
SCALE = 1.0 / math.sqrt(HD)
C2 = SCALE * math.log2(math.e)
FAR = 128.0
SEGS = 8
VMEM_BYTES = 12 * 1024 * 1024
ALL_VMEM = 63_000_000
F32 = jnp.float32
BF16 = jnp.bfloat16
WHOLE = pl.BlockSpec(memory_space=pltpu.VMEM)
ANYWHERE = pl.BlockSpec(memory_space=pl.ANY)


def call(
    kernel, name, out_shape, args, scratch=(), anywhere=0, vmem=VMEM_BYTES, flops=0, moved=0, exps=0
):
    return pl.pallas_call(
        kernel,
        out_shape=out_shape,
        in_specs=[ANYWHERE] * anywhere + [WHOLE] * (len(args) - anywhere),
        out_specs=jax.tree.map(lambda _: WHOLE, out_shape),
        scratch_shapes=list(scratch),
        compiler_params=pltpu.CompilerParams(vmem_limit_bytes=vmem),
        cost_estimate=pl.CostEstimate(flops=flops, bytes_accessed=moved, transcendentals=exps),
        name=name,
    )(*args)


def shape(dims, dtype):
    return jax.ShapeDtypeStruct(dims, dtype)


def dot_nn(a, b):
    return lax.dot_general(a, b, (((1,), (0,)), ((), ())), preferred_element_type=F32)


def dot_nt(a, b):
    return lax.dot_general(a, b, (((1,), (1,)), ((), ())), preferred_element_type=F32)


def write_block(first, second, seg_ref, out_ref):
    for h in range(HP):
        cols = slice(h * HD, (h + 1) * HD)
        out_ref[h * TB : (h + 1) * TB, :] = first[:, cols]
        out_ref[(HP + h) * TB : (HP + h + 1) * TB, :] = second[:, cols]
    out_ref[PR : PR + SR, :] = jnp.broadcast_to(seg_ref[...].astype(F32), (SR, TB)).astype(BF16)


def fetch(sources, held, sems):
    copies = [pltpu.make_async_copy(a, b, sems.at[i]) for i, (a, b) in enumerate(zip(sources, held))]
    for copy in copies:
        copy.start()
    for copy in copies:
        copy.wait()


def pack_kernel(*refs):
    sources, (kv_ref, qg_ref), (*held, sems) = refs[:6], refs[6:8], refs[8:]
    fetch(sources, held, sems)
    seg, key, value, query, grad, weight = held
    write_block(key[...], value[...], seg, kv_ref)
    write_block(query[...], dot_nt(grad[...], weight[...]).astype(BF16), seg, qg_ref)


def pack(*args):
    block = shape((PR + SR, HD), BF16)
    scratch = [pltpu.VMEM(a.shape, a.dtype) for a in args] + [pltpu.SemaphoreType.DMA((len(args),))]
    return call(pack_kernel, "pack", (block, block), args, scratch, len(args), ALL_VMEM)


def fill_marks(part_refs, mark_ref, for_keys):
    place = lax.broadcasted_iota(jnp.int32, (TB, TB), 0).astype(F32)
    start = 0
    for part_ref in part_refs:
        for b in range(part_ref.shape[0]):
            seg = part_ref[b, PR : PR + SR, :][0:1].astype(F32)
            if for_keys:
                marks = jnp.where((place != seg) & (place < SEGS), -FAR, 0.0)
            else:
                marks = jnp.where(place == seg, FAR, 0.0)
            mark_ref[start : start + TB, :] = jnp.transpose(marks).astype(BF16)
            start += TB


def head_rows(refs, slot):
    return jnp.concatenate(
        [
            ref[:, slot * TB : (slot + 1) * TB, :].reshape(ref.shape[0] * TB, HD)
            for ref in refs
        ],
        axis=0,
    )


STEP = 2
ROWS = STEP * TB


def merge(first, second):
    top = jnp.maximum(first[0], second[0])
    norm = top + jnp.log2(jnp.exp2(first[0] - top) + jnp.exp2(second[0] - top))
    delta = jnp.exp2(first[0] - norm) * first[1] + jnp.exp2(second[0] - norm) * second[1]
    return norm, delta


def chunk_rows(ref, slot):
    return ref[:, slot * TB : (slot + 1) * TB, :].reshape(ROWS, HD)


def stats_part(tasks, qmark, cols_ref, rows_ref):
    cols_ref[...] = jnp.zeros_like(cols_ref)
    for h in range(HP):
        for key_refs, kmarks, chunks in tasks:
            marks = jnp.concatenate([m[...] for m in kmarks], axis=0)
            k = jnp.concatenate([head_rows(key_refs, h), marks], axis=1)
            v = head_rows(key_refs, HP + h)
            for chunk, i in chunks:
                here = slice(i * ROWS, (i + 1) * ROWS)
                q, g = chunk_rows(chunk, h), chunk_rows(chunk, HP + h)
                scores = dot_nt(jnp.concatenate([q, qmark[here, :]], axis=1), k)
                top = jnp.max(scores, axis=1, keepdims=True)
                e = jnp.exp2((scores - top) * C2)
                cols_ref[here, 3 * h : 3 * h + 1] = top
                cols_ref[here, 3 * h + 1 : 3 * h + 2] = jnp.sum(e, axis=1, keepdims=True)
                cols_ref[here, 3 * h + 2 : 3 * h + 3] = jnp.sum(
                    e * dot_nt(g, v), axis=1, keepdims=True
                )
    found = jnp.transpose(cols_ref[...])
    rows_ref[...] = jnp.zeros_like(rows_ref)
    for h in range(HP):
        top, total, delta = (found[r : r + 1, :] for r in range(3 * h, 3 * h + 3))
        rows_ref[2 * h : 2 * h + 1, :] = top * C2 + jnp.log2(total)
        rows_ref[2 * h + 1 : 2 * h + 2, :] = delta / total


def rows_to_cols(rows_ref, cols_ref):
    rows = rows_ref[...]
    rest = jnp.zeros((HD - rows.shape[0], rows.shape[1]), F32)
    cols_ref[...] = jnp.transpose(jnp.concatenate([rows, rest], axis=0))


def early_stats_kernel(*refs):
    *chunks, key_ref, cols_ref, rows_ref, qmark, kmark = refs
    fill_marks(chunks, qmark, False)
    fill_marks((key_ref,), kmark, True)
    chunks = [(chunk, i) for i, chunk in enumerate(chunks)]
    stats_part([((key_ref,), (kmark,), chunks)], qmark, cols_ref, rows_ref)
    rows_to_cols(rows_ref, cols_ref)


def all_stats_kernel(early, count, *refs):
    chunks, refs = refs[:count], refs[count:]
    ko_ref, kx_ref, kmark_o, early_mark, before_ref, cols_ref, rows_ref, qmark, kmark_x = refs
    fill_marks((kx_ref,), kmark_x, True)
    late = [i for i in range(count) if i not in early]
    for j, i in enumerate(early):
        qmark[i * ROWS : (i + 1) * ROWS, :] = early_mark[j * ROWS : (j + 1) * ROWS, :]
    for i in late:
        fill_marks((chunks[i],), qmark.at[i * ROWS : (i + 1) * ROWS, :], False)
    tasks = [
        ((kx_ref,), (kmark_x,), [(chunks[i], i) for i in early]),
        ((ko_ref, kx_ref), (kmark_o, kmark_x), [(chunks[i], i) for i in late]),
    ]
    stats_part(tasks, qmark, cols_ref, rows_ref)
    for j, i in enumerate(early):
        then, here = slice(j * ROWS, (j + 1) * ROWS), slice(i * ROWS, (i + 1) * ROWS)
        for r in range(0, 2 * HP, 2):
            norm, delta = merge(
                (before_ref[r : r + 1, then], before_ref[r + 1 : r + 2, then]),
                (rows_ref[r : r + 1, here], rows_ref[r + 1 : r + 2, here]),
            )
            rows_ref[r : r + 1, here] = norm
            rows_ref[r + 1 : r + 2, here] = delta
    rows_to_cols(rows_ref, cols_ref)


def early_stats(chunks, key):
    n, m = len(chunks) * ROWS, key.shape[0] * TB
    out = (shape((n, HD), F32), shape((8, n), F32), shape((n, HD), BF16), shape((m, HD), BF16))
    return call(early_stats_kernel, "stats_early", out, (*chunks, key))


def all_stats(early, chunks, *args):
    n, m = len(chunks) * ROWS, args[1].shape[0] * TB
    out = (shape((n, HD), F32), shape((8, n), F32), shape((n, HD), BF16), shape((m, HD), BF16))
    kernel = functools.partial(all_stats_kernel, early, len(chunks))
    return call(kernel, "stats_all", out, (*chunks, *args))


def forward_kernel(first, skips, parts, *refs):
    count = len(skips)
    chunks, keys, refs = refs[:count], refs[count : count + parts], refs[count + parts :]
    kmarks, (qmark, norm_ref, out_ref) = refs[:parts], refs[parts:]
    marks = jnp.concatenate([m[...] for m in kmarks], axis=0)
    for h in range(HP):
        k = head_rows(keys, h)
        v = head_rows(keys, HP + h)
        k_marked = jnp.concatenate([k, marks], axis=1)
        vk = jnp.concatenate([v, k], axis=1)
        for i, (chunk, skip) in enumerate(zip(chunks, skips)):
            here = slice(i * ROWS, (i + 1) * ROWS)
            there = slice((first + i) * ROWS, (first + i + 1) * ROWS)
            q, g = chunk_rows(chunk, h), chunk_rows(chunk, HP + h)
            scores = dot_nt(jnp.concatenate([q, qmark[there, :]], axis=1), k_marked[skip:])
            p = jnp.exp2(scores * C2 - norm_ref[there, 2 * h : 2 * h + 1])
            mix = p * dot_nt(g, v[skip:])
            out_ref[h, here, : 2 * HD] = dot_nn(p.astype(BF16), vk[skip:])
            out_ref[h, here, 2 * HD :] = dot_nn(mix.astype(BF16), k[skip:])


def forward(name, first, skips, chunks, keys, kmarks, qmark, cols, flops=0):
    n = len(chunks) * ROWS
    return call(
        functools.partial(forward_kernel, first, skips, len(keys)), name,
        shape((HP, n, 3 * HD), F32), (*chunks, *keys, *kmarks, qmark, cols), flops=flops,
    )


def pair_kernel(later_ref, *refs):
    del later_ref
    mine_ref, got_ref, out_ref = refs
    out_ref[...] = jnp.zeros_like(out_ref)
    for block in range(mine_ref.shape[1] // TB):
        mine = slice(block * TB, (block + 1) * TB)
        theirs = slice((block ^ 1) * TB, ((block ^ 1) + 1) * TB)
        for r in range(0, 2 * HP, 2):
            norm, delta = merge(
                (mine_ref[r : r + 1, mine], mine_ref[r + 1 : r + 2, mine]),
                (got_ref[r : r + 1, theirs], got_ref[r + 1 : r + 2, theirs]),
            )
            out_ref[r : r + 1, mine] = norm
            out_ref[r + 1 : r + 2, mine] = delta


def pair(later, mine, got):
    return call(pair_kernel, "pair_rows", shape(mine.shape, F32), (later, mine, got), anywhere=1)


def whole_kernel(steps, later_ref, *refs):
    del later_ref
    *members, stat_ref = refs
    stat_ref[...] = jnp.zeros_like(stat_ref)
    for i, mine in enumerate(steps):
        here = slice(i * ROWS, (i + 1) * ROWS)
        found = []
        for member, step in zip(members, steps):
            at = steps.index((mine - step) % len(steps)) * ROWS
            found.append(member[:, at : at + ROWS])
        for r in range(0, 2 * HP, 2):
            norm, delta = functools.reduce(merge, [(f[r : r + 1], f[r + 1 : r + 2]) for f in found])
            stat_ref[r : r + 1, here] = norm
            stat_ref[r + 1 : r + 2, here] = delta


def whole(steps, members, later):
    out = shape(members[0].shape, F32)
    return call(functools.partial(whole_kernel, steps), "whole_rows", out, (later, *members), anywhere=1)


def share_kernel(chunks, early, later_ref, stat_ref, rows_ref, early_rows, *refs):
    del later_ref
    outs, early_out, sends, partners = refs[:2], refs[2], refs[3 : 3 + chunks], refs[3 + chunks :]
    partners = [None] * (chunks - len(partners)) + list(partners)
    rows = []
    for r in range(0, 2 * HP, 2):
        rows.append(jnp.exp2(rows_ref[r : r + 1, :] - stat_ref[r : r + 1, :]))
        rows.append(stat_ref[r + 1 : r + 2, :])
        parts = [jnp.zeros((1, ROWS), F32)] * chunks
        for j, i in enumerate(early):
            then, here = slice(j * ROWS, (j + 1) * ROWS), slice(i * ROWS, (i + 1) * ROWS)
            parts[i] = jnp.exp2(early_rows[r : r + 1, then] - stat_ref[r : r + 1, here])
        rows.append(jnp.concatenate(parts, axis=1))
    rows.append(jnp.zeros((TB - 3 * HP, chunks * ROWS), F32))
    cols = jnp.transpose(jnp.concatenate(rows, axis=0))
    for i, send_ref in enumerate(sends):
        here = slice(i * ROWS, (i + 1) * ROWS)
        out_ref, start = outs[i // (chunks // 2)], i % (chunks // 2) * ROWS
        there = slice(start, start + ROWS)
        for h in range(HP):
            share, delta, early_share = (cols[here, 3 * h + c : 3 * h + c + 1] for c in range(3))
            attn, plain, mixed = (
                share * out_ref[h, there, c * HD : (c + 1) * HD] for c in range(3)
            )
            if i in early:
                then = slice(early.index(i) * ROWS, (early.index(i) + 1) * ROWS)
                more = [
                    early_share * early_out[h, then, c * HD : (c + 1) * HD] for c in range(3)
                ]
                attn, plain, mixed = attn + more[0], plain + more[1], mixed + more[2]
            attn = attn.astype(BF16)
            grad = (SCALE * (mixed - delta * plain)).astype(BF16)
            for slot, value in ((h, attn), (HP + h, grad)):
                there_rows = slice(slot * TB, (slot + 1) * TB)
                send_ref[0, there_rows, :] = value[:TB]
                if partners[i] is None:
                    send_ref[1, there_rows, :] = value[TB:]
                else:
                    partners[i][there_rows, :] = value[TB:]


def shares(chunks, far, early, later, *args):
    out = (shape((STEP, PR, HD), BF16),) * (chunks - far) + (shape((1, PR, HD), BF16),) * far
    out += (shape((PR, HD), BF16),) * far
    return call(
        functools.partial(share_kernel, chunks, early), "share_rows", out, (later, *args),
        anywhere=1, moved=4 * 2**20,
    )


def backward_kernel(count, k_ref, *refs):
    chunks, (kmark, qmark, stat_ref, send_ref) = refs[:count], refs[count:]
    marks = qmark[...]
    for h in range(HP):
        q = head_rows(chunks, h)
        g = head_rows(chunks, HP + h)
        q_marked = jnp.concatenate([q, marks], axis=1)
        norm, delta = (stat_ref[r : r + 1, :] for r in (2 * h, 2 * h + 1))

        for i in range(k_ref.shape[0] // STEP):
            here = slice(i * ROWS, (i + 1) * ROWS)
            these = slice(i * STEP, (i + 1) * STEP)
            k, v = (
                k_ref[these, slot * TB : (slot + 1) * TB, :].reshape(ROWS, HD)
                for slot in (h, HP + h)
            )
            scores = dot_nt(jnp.concatenate([k, kmark[here, :]], axis=1), q_marked)
            probs = jnp.exp2(scores * C2 - norm)
            change = probs * (dot_nt(v, g) - delta)
            grad_k = (dot_nn(change.astype(BF16), q) * SCALE).astype(BF16)
            grad_v = dot_nn(probs.astype(BF16), g).astype(BF16)
            send_ref[these, h * TB : (h + 1) * TB, :] = grad_k.reshape(STEP, TB, HD)
            send_ref[these, (HP + h) * TB : (HP + h + 1) * TB, :] = grad_v.reshape(STEP, TB, HD)


def backward(name, k, chunks, kmark, qmark, stat):
    n, m = len(chunks) * ROWS, k.shape[0] * TB
    args = (k, *chunks, kmark, qmark, stat)
    return call(
        functools.partial(backward_kernel, len(chunks)), name,
        shape((k.shape[0], PR, HD), BF16), args,
        flops=10 * n * m * 2 * HD * HP, moved=8 * 2**20, exps=n * m * HP,
    )


def partner_sum_kernel(later_ref, *refs):
    del later_ref
    refs[-1][...] = sum(ref[1].astype(F32) for ref in refs[:-1]).astype(BF16)


def partner_sum(parts, later):
    return call(
        partner_sum_kernel, "sum_partner", shape((PR, HD), BF16), (later, *parts), anywhere=1,
        moved=len(parts) * PR * HD * 2,
    )


def far_sum_kernel(later_ref, mine_ref, got_ref, out_ref):
    del later_ref
    out_ref[...] = (mine_ref[0].astype(F32) + got_ref[...].astype(F32)).astype(BF16)


def far_sum(mine, got, later):
    args = (later, mine, got)
    return call(far_sum_kernel, "sum_far", shape((PR, HD), BF16), args, anywhere=1)


def add_kernel(later_ref, own_ref, got_ref, *out_refs):
    del later_ref
    for j, out_ref in enumerate(out_refs):
        out_ref[...] = (own_ref[j].astype(F32) + got_ref[j].astype(F32)).astype(BF16)


def add(own, got, name, later):
    out = tuple(shape(own.shape[1:], BF16) for _ in range(own.shape[0]))
    args = (later, own, got)
    return call(add_kernel, name, out, args, anywhere=1, flops=own.size, moved=6 * own.size)


def sum_kernel(skip, *refs):
    parts, (first_ref, second_ref) = refs[skip:-2], refs[-2:]
    parts = [part[0] if len(part.shape) == 3 else part[...] for part in parts]
    total = sum(part.astype(F32) for part in parts).astype(BF16)
    for h in range(HP):
        cols = slice(h * HD, (h + 1) * HD)
        first_ref[:, cols] = total[h * TB : (h + 1) * TB, :]
        second_ref[:, cols] = total[(HP + h) * TB : (HP + h + 1) * TB, :]


def sum_parts(parts, name, later=()):
    out = shape((TB, HP * HD), BF16)
    size = sum(p.size for p in parts)
    kernel, args = functools.partial(sum_kernel, len(later)), (*later, *parts)
    return call(kernel, name, (out, out), args, anywhere=len(later), flops=size, moved=2 * size)


def project_kernel(own_ref, other_ref, own_weight, other_weight, out_ref, token_ref):
    token_ref[...] = jnp.zeros_like(token_ref)
    out_ref[...] = (
        dot_nn(own_ref[...], own_weight[...]) + dot_nn(other_ref[...], other_weight[...])
    ).astype(BF16)


def project(own, other, own_weight, other_weight):
    width = own_weight.shape[1]
    return call(
        project_kernel, "project", (shape((TB, width), BF16), shape((8, HD), F32)),
        (own, other, own_weight, other_weight),
        flops=4 * own.size * width, moved=4 * own_weight.size,
    )


class Places:
    def __init__(self, n_row, n_col):
        self.n_row, self.n_col = n_row, n_col
        self.ny, self.nz = n_col // 2, n_row // 2

    def of(self, index):
        row, col = divmod(index, self.n_col)
        low, z = divmod(row, self.nz)
        y, high = divmod(col, 2)
        return high, low, y, z

    def index(self, high, low, y, z):
        return (low * self.nz + z) * self.n_col + y * 2 + high

    def send(self, array, move):
        pairs = []
        for i in range(self.n_row * self.n_col):
            for core in range(2):
                target = self.index(*move(core, *self.of(i)))
                pairs.append((2 * i + core, 2 * target + core))
        return lax.ppermute(array, ("row", "col", "head"), pairs)

    def along_y(self, array, by):
        return self.send(array, lambda core, high, low, y, z: (high, low, (y + by) % self.ny, z))

    def along_z(self, array, by):
        return self.send(array, lambda core, high, low, y, z: (high, low, y, (z + by) % self.nz))

    def query_partner(self, array):
        return self.send(array, lambda core, high, low, y, z: (high ^ 1 ^ core, low ^ 1, y, z))

    def query_partner_along_y(self, array, by):
        return self.send(
            array,
            lambda core, high, low, y, z: (high ^ 1 ^ core, low ^ 1, (y + by) % self.ny, z),
        )

    def key_partner(self, array):
        return self.send(array, lambda core, high, low, y, z: (high ^ core, low ^ 1, y, z))


def shifts(n):
    return [0] + sorted(range(1, n), key=lambda d: min(d, n - d))


def on_device(places, query, key, value, segment_ids, out_weight, grad_output):
    swap = [(0, 1), (1, 0)]
    y_shifts, z_shifts = shifts(places.ny), shifts(places.nz)
    seg = segment_ids.reshape(1, TB)

    kv, qg = pack(seg, key, value, query, grad_output, out_weight)
    pair0 = jnp.stack([qg, places.query_partner(qg)])
    far = [d for d in y_shifts if 1 < d == places.ny - d]
    near = [d for d in y_shifts[1:] if d not in far]
    chunks = [pair0] + [places.along_y(pair0, d) for d in near]
    far_blocks = [places.along_y(qg, d) for d in far]
    far_partner_blocks = [places.query_partner_along_y(qg, d) for d in far]
    chunks += [jnp.stack(pair) for pair in zip(far_blocks, far_partner_blocks)]
    key_blocks = [places.along_z(kv, d) for d in z_shifts[1:]]
    (kv, *key_blocks), *_ = lax.optimization_barrier(
        ((kv, *key_blocks), pair0, *far_blocks, *far_partner_blocks)
    )
    ko = jnp.stack([kv] + key_blocks)
    kx = places.key_partner(ko)
    other_weight = lax.ppermute(out_weight, "head", swap)

    count = len(chunks)
    early = [i for i in range(count) if not 1 <= i <= len(near)]
    some = [chunks[i] for i in early]
    early_cols, early_rows, early_mark, kmark_o = early_stats(some, ko)
    early_out = forward(
        "forward_early", 0, [0] * len(early), some, [ko], [kmark_o], early_mark, early_cols
    )
    early_rows, _ = lax.optimization_barrier((early_rows, early_out))
    cols, rows, qmark, kmark_x = all_stats(early, chunks, ko, kx, kmark_o, early_mark, early_rows)
    got = places.query_partner(rows)
    halves = []
    for name, first in (("forward_near", 0), ("forward_far", count // 2)):
        if halves:
            pair_rows = pair(halves[0], rows, got)
            members = [pair_rows] + [places.along_y(pair_rows, d) for d in y_shifts[1:]]
        some = chunks[first : first + count // 2]
        skips = [ko.shape[0] * TB * (first + i in early) for i in range(len(some))]
        keys, kmarks = (ko, kx), (kmark_o, kmark_x)
        halves.append(forward(name, first, skips, some, keys, kmarks, qmark, cols, 3 * 10**9))
    stat = whole(y_shifts, members, halves[1])
    key_partner = backward("backward_partner", kx, chunks, kmark_x, qmark, stat)
    key_got = places.key_partner(key_partner)

    made = shares(count, len(far), early, key_partner, stat, rows, early_rows, *halves, early_out)
    sends, far_partners = made[:count], made[count:]
    row_parts = [sends[0]] + [places.along_y(part, -d) for part, d in zip(sends[1:], near)]
    far_parts = sends[len(row_parts) :]
    far_got = [places.query_partner(far_rows) for far_rows in far_partners]
    key_own = backward("backward_own", ko, chunks, kmark_o, qmark, stat)
    far_parts = [
        places.along_y(far_sum(part, got, key_own), -d)
        for part, got, d in zip(far_parts, far_got, far)
    ]

    key_parts = add(key_own, key_got, "add_keys", stat)
    key_parts = [key_parts[0]] + [
        places.along_z(part, -d) for part, d in zip(key_parts[1:], z_shifts[1:])
    ]
    row_got = places.query_partner(partner_sum(row_parts, key_parts[0]))
    attn, grad_queries = sum_parts(row_parts + far_parts + [row_got], "sum_rows")
    other_attn = lax.ppermute(attn, "head", swap)
    mixed_output, token = project(attn, other_attn, out_weight, other_weight)
    grad_keys, grad_values = sum_parts(key_parts, "sum_keys", (token,))
    return (mixed_output, grad_queries, grad_keys, grad_values)


def solution(mesh):
    tokens = P(("row", "col"))
    heads = P(("row", "col"), "head")
    whole = P(("row", "col"), None)
    places = Places(mesh.shape["row"], mesh.shape["col"])
    return jax.shard_map(
        functools.partial(on_device, places),
        mesh=mesh,
        in_specs=(heads, heads, heads, tokens, P("head", None), whole),
        out_specs=(whole, heads, heads, heads),
        check_vma=False,
    )
```

```python
import functools
import math

import jax
import jax.numpy as jnp
from jax import lax
from jax.experimental import pallas as pl
from jax.experimental.pallas import tpu as pltpu
from jax.sharding import PartitionSpec as P

HD = 128
TB = 128
HP = 3
PR = 2 * HP * TB
SR = 16
SCALE = 1.0 / math.sqrt(HD)
C2 = SCALE * math.log2(math.e)
FAR = 128.0
SEGS = 8
VMEM_BYTES = 12 * 1024 * 1024
ALL_VMEM = 63_000_000
F32 = jnp.float32
BF16 = jnp.bfloat16
WHOLE = pl.BlockSpec(memory_space=pltpu.VMEM)
ANYWHERE = pl.BlockSpec(memory_space=pl.ANY)


def call(
    kernel, name, out_shape, args, scratch=(), anywhere=0, vmem=VMEM_BYTES, flops=0, moved=0, exps=0
):
    return pl.pallas_call(
        kernel,
        out_shape=out_shape,
        in_specs=[ANYWHERE] * anywhere + [WHOLE] * (len(args) - anywhere),
        out_specs=jax.tree.map(lambda _: WHOLE, out_shape),
        scratch_shapes=list(scratch),
        compiler_params=pltpu.CompilerParams(vmem_limit_bytes=vmem),
        cost_estimate=pl.CostEstimate(flops=flops, bytes_accessed=moved, transcendentals=exps),
        name=name,
    )(*args)


def shape(dims, dtype):
    return jax.ShapeDtypeStruct(dims, dtype)


def dot_nn(a, b):
    return lax.dot_general(a, b, (((1,), (0,)), ((), ())), preferred_element_type=F32)


def dot_nt(a, b):
    return lax.dot_general(a, b, (((1,), (1,)), ((), ())), preferred_element_type=F32)


def write_block(first, second, seg_ref, out_ref):
    for h in range(HP):
        cols = slice(h * HD, (h + 1) * HD)
        out_ref[h * TB : (h + 1) * TB, :] = first[:, cols]
        out_ref[(HP + h) * TB : (HP + h + 1) * TB, :] = second[:, cols]
    out_ref[PR : PR + SR, :] = jnp.broadcast_to(seg_ref[...].astype(F32), (SR, TB)).astype(BF16)


def fetch(sources, held, sems):
    copies = [pltpu.make_async_copy(a, b, sems.at[i]) for i, (a, b) in enumerate(zip(sources, held))]
    for copy in copies:
        copy.start()
    for copy in copies:
        copy.wait()


def pack_kernel(*refs):
    sources, (kv_ref, qg_ref), (*held, sems) = refs[:6], refs[6:8], refs[8:]
    fetch(sources, held, sems)
    seg, key, value, query, grad, weight = held
    write_block(key[...], value[...], seg, kv_ref)
    write_block(query[...], dot_nt(grad[...], weight[...]).astype(BF16), seg, qg_ref)


def pack(*args):
    block = shape((PR + SR, HD), BF16)
    scratch = [pltpu.VMEM(a.shape, a.dtype) for a in args] + [pltpu.SemaphoreType.DMA((len(args),))]
    return call(pack_kernel, "pack", (block, block), args, scratch, len(args), ALL_VMEM)


def fill_marks(part_refs, mark_ref, for_keys):
    place = lax.broadcasted_iota(jnp.int32, (TB, TB), 0).astype(F32)
    start = 0
    for part_ref in part_refs:
        for b in range(part_ref.shape[0]):
            seg = part_ref[b, PR : PR + SR, :][0:1].astype(F32)
            if for_keys:
                marks = jnp.where((place != seg) & (place < SEGS), -FAR, 0.0)
            else:
                marks = jnp.where(place == seg, FAR, 0.0)
            mark_ref[start : start + TB, :] = jnp.transpose(marks).astype(BF16)
            start += TB


def head_rows(refs, slot):
    return jnp.concatenate(
        [
            ref[:, slot * TB : (slot + 1) * TB, :].reshape(ref.shape[0] * TB, HD)
            for ref in refs
        ],
        axis=0,
    )


STEP = 2
ROWS = STEP * TB


def merge(first, second):
    top = jnp.maximum(first[0], second[0])
    norm = top + jnp.log2(jnp.exp2(first[0] - top) + jnp.exp2(second[0] - top))
    delta = jnp.exp2(first[0] - norm) * first[1] + jnp.exp2(second[0] - norm) * second[1]
    return norm, delta


def chunk_rows(ref, slot):
    return ref[:, slot * TB : (slot + 1) * TB, :].reshape(ROWS, HD)


def stats_part(tasks, qmark, cols_ref, rows_ref):
    cols_ref[...] = jnp.zeros_like(cols_ref)
    for h in range(HP):
        for key_refs, kmarks, chunks in tasks:
            marks = jnp.concatenate([m[...] for m in kmarks], axis=0)
            k = jnp.concatenate([head_rows(key_refs, h), marks], axis=1)
            v = head_rows(key_refs, HP + h)
            for chunk, i in chunks:
                here = slice(i * ROWS, (i + 1) * ROWS)
                q, g = chunk_rows(chunk, h), chunk_rows(chunk, HP + h)
                scores = dot_nt(jnp.concatenate([q, qmark[here, :]], axis=1), k)
                top = jnp.max(scores, axis=1, keepdims=True)
                e = jnp.exp2((scores - top) * C2)
                cols_ref[here, 3 * h : 3 * h + 1] = top
                cols_ref[here, 3 * h + 1 : 3 * h + 2] = jnp.sum(e, axis=1, keepdims=True)
                cols_ref[here, 3 * h + 2 : 3 * h + 3] = jnp.sum(
                    e * dot_nt(g, v), axis=1, keepdims=True
                )
    found = jnp.transpose(cols_ref[...])
    rows_ref[...] = jnp.zeros_like(rows_ref)
    for h in range(HP):
        top, total, delta = (found[r : r + 1, :] for r in range(3 * h, 3 * h + 3))
        rows_ref[2 * h : 2 * h + 1, :] = top * C2 + jnp.log2(total)
        rows_ref[2 * h + 1 : 2 * h + 2, :] = delta / total


def rows_to_cols(rows_ref, cols_ref):
    rows = rows_ref[...]
    rest = jnp.zeros((HD - rows.shape[0], rows.shape[1]), F32)
    cols_ref[...] = jnp.transpose(jnp.concatenate([rows, rest], axis=0))


def early_stats_kernel(*refs):
    *chunks, key_ref, cols_ref, rows_ref, qmark, kmark = refs
    fill_marks(chunks, qmark, False)
    fill_marks((key_ref,), kmark, True)
    chunks = [(chunk, i) for i, chunk in enumerate(chunks)]
    stats_part([((key_ref,), (kmark,), chunks)], qmark, cols_ref, rows_ref)
    rows_to_cols(rows_ref, cols_ref)


def all_stats_kernel(early, count, *refs):
    chunks, refs = refs[:count], refs[count:]
    ko_ref, kx_ref, kmark_o, early_mark, before_ref, cols_ref, rows_ref, qmark, kmark_x = refs
    fill_marks((kx_ref,), kmark_x, True)
    late = [i for i in range(count) if i not in early]
    for j, i in enumerate(early):
        qmark[i * ROWS : (i + 1) * ROWS, :] = early_mark[j * ROWS : (j + 1) * ROWS, :]
    for i in late:
        fill_marks((chunks[i],), qmark.at[i * ROWS : (i + 1) * ROWS, :], False)
    tasks = [
        ((kx_ref,), (kmark_x,), [(chunks[i], i) for i in early]),
        ((ko_ref, kx_ref), (kmark_o, kmark_x), [(chunks[i], i) for i in late]),
    ]
    stats_part(tasks, qmark, cols_ref, rows_ref)
    for j, i in enumerate(early):
        then, here = slice(j * ROWS, (j + 1) * ROWS), slice(i * ROWS, (i + 1) * ROWS)
        for r in range(0, 2 * HP, 2):
            norm, delta = merge(
                (before_ref[r : r + 1, then], before_ref[r + 1 : r + 2, then]),
                (rows_ref[r : r + 1, here], rows_ref[r + 1 : r + 2, here]),
            )
            rows_ref[r : r + 1, here] = norm
            rows_ref[r + 1 : r + 2, here] = delta
    rows_to_cols(rows_ref, cols_ref)


def early_stats(chunks, key):
    n, m = len(chunks) * ROWS, key.shape[0] * TB
    out = (shape((n, HD), F32), shape((8, n), F32), shape((n, HD), BF16), shape((m, HD), BF16))
    return call(early_stats_kernel, "stats_early", out, (*chunks, key))


def all_stats(early, chunks, *args):
    n, m = len(chunks) * ROWS, args[1].shape[0] * TB
    out = (shape((n, HD), F32), shape((8, n), F32), shape((n, HD), BF16), shape((m, HD), BF16))
    kernel = functools.partial(all_stats_kernel, early, len(chunks))
    return call(kernel, "stats_all", out, (*chunks, *args))


def forward_kernel(first, skips, parts, *refs):
    count = len(skips)
    chunks, keys, refs = refs[:count], refs[count : count + parts], refs[count + parts :]
    kmarks, (qmark, norm_ref, out_ref) = refs[:parts], refs[parts:]
    marks = jnp.concatenate([m[...] for m in kmarks], axis=0)
    for h in range(HP):
        k = head_rows(keys, h)
        v = head_rows(keys, HP + h)
        k_marked = jnp.concatenate([k, marks], axis=1)
        vk = jnp.concatenate([v, k], axis=1)
        for i, (chunk, skip) in enumerate(zip(chunks, skips)):
            here = slice(i * ROWS, (i + 1) * ROWS)
            there = slice((first + i) * ROWS, (first + i + 1) * ROWS)
            q, g = chunk_rows(chunk, h), chunk_rows(chunk, HP + h)
            scores = dot_nt(jnp.concatenate([q, qmark[there, :]], axis=1), k_marked[skip:])
            p = jnp.exp2(scores * C2 - norm_ref[there, 2 * h : 2 * h + 1])
            mix = p * dot_nt(g, v[skip:])
            out_ref[h, here, : 2 * HD] = dot_nn(p.astype(BF16), vk[skip:])
            out_ref[h, here, 2 * HD :] = dot_nn(mix.astype(BF16), k[skip:])


def forward(name, first, skips, chunks, keys, kmarks, qmark, cols, flops=0):
    n = len(chunks) * ROWS
    return call(
        functools.partial(forward_kernel, first, skips, len(keys)), name,
        shape((HP, n, 3 * HD), F32), (*chunks, *keys, *kmarks, qmark, cols), flops=flops,
    )


def pair_kernel(later_ref, *refs):
    del later_ref
    mine_ref, got_ref, out_ref = refs
    out_ref[...] = jnp.zeros_like(out_ref)
    for block in range(mine_ref.shape[1] // TB):
        mine = slice(block * TB, (block + 1) * TB)
        theirs = slice((block ^ 1) * TB, ((block ^ 1) + 1) * TB)
        for r in range(0, 2 * HP, 2):
            norm, delta = merge(
                (mine_ref[r : r + 1, mine], mine_ref[r + 1 : r + 2, mine]),
                (got_ref[r : r + 1, theirs], got_ref[r + 1 : r + 2, theirs]),
            )
            out_ref[r : r + 1, mine] = norm
            out_ref[r + 1 : r + 2, mine] = delta


def pair(later, mine, got):
    return call(pair_kernel, "pair_rows", shape(mine.shape, F32), (later, mine, got), anywhere=1)


def whole_kernel(steps, later_ref, *refs):
    del later_ref
    *members, stat_ref = refs
    stat_ref[...] = jnp.zeros_like(stat_ref)
    for i, mine in enumerate(steps):
        here = slice(i * ROWS, (i + 1) * ROWS)
        found = []
        for member, step in zip(members, steps):
            at = steps.index((mine - step) % len(steps)) * ROWS
            found.append(member[:, at : at + ROWS])
        for r in range(0, 2 * HP, 2):
            norm, delta = functools.reduce(merge, [(f[r : r + 1], f[r + 1 : r + 2]) for f in found])
            stat_ref[r : r + 1, here] = norm
            stat_ref[r + 1 : r + 2, here] = delta


def whole(steps, members, later):
    out = shape(members[0].shape, F32)
    return call(functools.partial(whole_kernel, steps), "whole_rows", out, (later, *members), anywhere=1)


def share_kernel(chunks, early, later_ref, stat_ref, rows_ref, early_rows, *refs):
    del later_ref
    outs, early_out, sends, partners = refs[:2], refs[2], refs[3 : 3 + chunks], refs[3 + chunks :]
    partners = [None] * (chunks - len(partners)) + list(partners)
    rows = []
    for r in range(0, 2 * HP, 2):
        rows.append(jnp.exp2(rows_ref[r : r + 1, :] - stat_ref[r : r + 1, :]))
        rows.append(stat_ref[r + 1 : r + 2, :])
        parts = [jnp.zeros((1, ROWS), F32)] * chunks
        for j, i in enumerate(early):
            then, here = slice(j * ROWS, (j + 1) * ROWS), slice(i * ROWS, (i + 1) * ROWS)
            parts[i] = jnp.exp2(early_rows[r : r + 1, then] - stat_ref[r : r + 1, here])
        rows.append(jnp.concatenate(parts, axis=1))
    rows.append(jnp.zeros((TB - 3 * HP, chunks * ROWS), F32))
    cols = jnp.transpose(jnp.concatenate(rows, axis=0))
    for i, send_ref in enumerate(sends):
        here = slice(i * ROWS, (i + 1) * ROWS)
        out_ref, start = outs[i // (chunks // 2)], i % (chunks // 2) * ROWS
        there = slice(start, start + ROWS)
        for h in range(HP):
            share, delta, early_share = (cols[here, 3 * h + c : 3 * h + c + 1] for c in range(3))
            attn, plain, mixed = (
                share * out_ref[h, there, c * HD : (c + 1) * HD] for c in range(3)
            )
            if i in early:
                then = slice(early.index(i) * ROWS, (early.index(i) + 1) * ROWS)
                more = [
                    early_share * early_out[h, then, c * HD : (c + 1) * HD] for c in range(3)
                ]
                attn, plain, mixed = attn + more[0], plain + more[1], mixed + more[2]
            attn = attn.astype(BF16)
            grad = (SCALE * (mixed - delta * plain)).astype(BF16)
            for slot, value in ((h, attn), (HP + h, grad)):
                there_rows = slice(slot * TB, (slot + 1) * TB)
                send_ref[0, there_rows, :] = value[:TB]
                if partners[i] is None:
                    send_ref[1, there_rows, :] = value[TB:]
                else:
                    partners[i][there_rows, :] = value[TB:]


def shares(chunks, far, early, later, *args):
    out = (shape((STEP, PR, HD), BF16),) * (chunks - far) + (shape((1, PR, HD), BF16),) * far
    out += (shape((PR, HD), BF16),) * far
    return call(
        functools.partial(share_kernel, chunks, early), "share_rows", out, (later, *args),
        anywhere=1, moved=4 * 2**20,
    )


def backward_kernel(count, k_ref, *refs):
    chunks, (kmark, qmark, stat_ref, send_ref) = refs[:count], refs[count:]
    marks = qmark[...]
    for h in range(HP):
        q = head_rows(chunks, h)
        g = head_rows(chunks, HP + h)
        q_marked = jnp.concatenate([q, marks], axis=1)
        norm, delta = (stat_ref[r : r + 1, :] for r in (2 * h, 2 * h + 1))

        for i in range(k_ref.shape[0] // STEP):
            here = slice(i * ROWS, (i + 1) * ROWS)
            these = slice(i * STEP, (i + 1) * STEP)
            k, v = (
                k_ref[these, slot * TB : (slot + 1) * TB, :].reshape(ROWS, HD)
                for slot in (h, HP + h)
            )
            scores = dot_nt(jnp.concatenate([k, kmark[here, :]], axis=1), q_marked)
            probs = jnp.exp2(scores * C2 - norm)
            change = probs * (dot_nt(v, g) - delta)
            grad_k = (dot_nn(change.astype(BF16), q) * SCALE).astype(BF16)
            grad_v = dot_nn(probs.astype(BF16), g).astype(BF16)
            send_ref[these, h * TB : (h + 1) * TB, :] = grad_k.reshape(STEP, TB, HD)
            send_ref[these, (HP + h) * TB : (HP + h + 1) * TB, :] = grad_v.reshape(STEP, TB, HD)


def backward(name, k, chunks, kmark, qmark, stat):
    n, m = len(chunks) * ROWS, k.shape[0] * TB
    args = (k, *chunks, kmark, qmark, stat)
    return call(
        functools.partial(backward_kernel, len(chunks)), name,
        shape((k.shape[0], PR, HD), BF16), args,
        flops=10 * n * m * 2 * HD * HP, moved=8 * 2**20, exps=n * m * HP,
    )


def partner_sum_kernel(later_ref, *refs):
    del later_ref
    refs[-1][...] = sum(ref[1].astype(F32) for ref in refs[:-1]).astype(BF16)


def partner_sum(parts, later):
    return call(
        partner_sum_kernel, "sum_partner", shape((PR, HD), BF16), (later, *parts), anywhere=1,
        moved=len(parts) * PR * HD * 2,
    )


def far_sum_kernel(later_ref, mine_ref, got_ref, out_ref):
    del later_ref
    out_ref[...] = (mine_ref[0].astype(F32) + got_ref[...].astype(F32)).astype(BF16)


def far_sum(mine, got, later):
    args = (later, mine, got)
    return call(far_sum_kernel, "sum_far", shape((PR, HD), BF16), args, anywhere=1)


def add_kernel(later_ref, own_ref, got_ref, *out_refs):
    del later_ref
    for j, out_ref in enumerate(out_refs):
        out_ref[...] = (own_ref[j].astype(F32) + got_ref[j].astype(F32)).astype(BF16)


def add(own, got, name, later):
    out = tuple(shape(own.shape[1:], BF16) for _ in range(own.shape[0]))
    args = (later, own, got)
    return call(add_kernel, name, out, args, anywhere=1, flops=own.size, moved=6 * own.size)


def sum_kernel(skip, *refs):
    parts, (first_ref, second_ref) = refs[skip:-2], refs[-2:]
    parts = [part[0] if len(part.shape) == 3 else part[...] for part in parts]
    total = sum(part.astype(F32) for part in parts).astype(BF16)
    for h in range(HP):
        cols = slice(h * HD, (h + 1) * HD)
        first_ref[:, cols] = total[h * TB : (h + 1) * TB, :]
        second_ref[:, cols] = total[(HP + h) * TB : (HP + h + 1) * TB, :]


def sum_parts(parts, name, later=()):
    out = shape((TB, HP * HD), BF16)
    size = sum(p.size for p in parts)
    kernel, args = functools.partial(sum_kernel, len(later)), (*later, *parts)
    return call(kernel, name, (out, out), args, anywhere=len(later), flops=size, moved=2 * size)


def project_kernel(own_ref, other_ref, own_weight, other_weight, out_ref, token_ref):
    token_ref[...] = jnp.zeros_like(token_ref)
    out_ref[...] = (
        dot_nn(own_ref[...], own_weight[...]) + dot_nn(other_ref[...], other_weight[...])
    ).astype(BF16)


def project(own, other, own_weight, other_weight):
    width = own_weight.shape[1]
    return call(
        project_kernel, "project", (shape((TB, width), BF16), shape((8, HD), F32)),
        (own, other, own_weight, other_weight),
        flops=4 * own.size * width, moved=4 * own_weight.size,
    )


class Places:
    def __init__(self, n_row, n_col):
        self.n_row, self.n_col = n_row, n_col
        self.ny, self.nz = n_col // 2, n_row // 2

    def of(self, index):
        row, col = divmod(index, self.n_col)
        low, z = divmod(row, self.nz)
        y, high = divmod(col, 2)
        return high, low, y, z

    def index(self, high, low, y, z):
        return (low * self.nz + z) * self.n_col + y * 2 + high

    def send(self, array, move):
        pairs = []
        for i in range(self.n_row * self.n_col):
            for core in range(2):
                target = self.index(*move(core, *self.of(i)))
                pairs.append((2 * i + core, 2 * target + core))
        return lax.ppermute(array, ("row", "col", "head"), pairs)

    def along_y(self, array, by):
        return self.send(array, lambda core, high, low, y, z: (high, low, (y + by) % self.ny, z))

    def along_z(self, array, by):
        return self.send(array, lambda core, high, low, y, z: (high, low, y, (z + by) % self.nz))

    def query_partner(self, array):
        return self.send(array, lambda core, high, low, y, z: (high ^ 1 ^ core, low ^ 1, y, z))

    def query_partner_along_y(self, array, by):
        return self.send(
            array,
            lambda core, high, low, y, z: (high ^ 1 ^ core, low ^ 1, (y + by) % self.ny, z),
        )

    def key_partner(self, array):
        return self.send(array, lambda core, high, low, y, z: (high ^ core, low ^ 1, y, z))


def shifts(n):
    return [0] + sorted(range(1, n), key=lambda d: min(d, n - d))


def on_device(places, query, key, value, segment_ids, out_weight, grad_output):
    swap = [(0, 1), (1, 0)]
    y_shifts, z_shifts = shifts(places.ny), shifts(places.nz)
    seg = segment_ids.reshape(1, TB)

    kv, qg = pack(seg, key, value, query, grad_output, out_weight)
    pair0 = jnp.stack([qg, places.query_partner(qg)])
    far = [d for d in y_shifts if 1 < d == places.ny - d]
    near = [d for d in y_shifts[1:] if d not in far]
    chunks = [pair0] + [places.along_y(pair0, d) for d in near]
    far_blocks = [places.along_y(qg, d) for d in far]
    far_partner_blocks = [places.query_partner_along_y(qg, d) for d in far]
    chunks += [jnp.stack(pair) for pair in zip(far_blocks, far_partner_blocks)]
    key_blocks = [places.along_z(kv, d) for d in z_shifts[1:]]
    (kv, *key_blocks), *_ = lax.optimization_barrier(
        ((kv, *key_blocks), pair0, *far_blocks, *far_partner_blocks)
    )
    ko = jnp.stack([kv] + key_blocks)
    kx = places.key_partner(ko)
    other_weight = lax.ppermute(out_weight, "head", swap)

    count = len(chunks)
    early = [i for i in range(count) if not 1 <= i <= len(near)]
    some = [chunks[i] for i in early]
    early_cols, early_rows, early_mark, kmark_o = early_stats(some, ko)
    early_out = forward(
        "forward_early", 0, [0] * len(early), some, [ko], [kmark_o], early_mark, early_cols
    )
    early_rows, _ = lax.optimization_barrier((early_rows, early_out))
    cols, rows, qmark, kmark_x = all_stats(early, chunks, ko, kx, kmark_o, early_mark, early_rows)
    got = places.query_partner(rows)
    halves = []
    for name, first in (("forward_near", 0), ("forward_far", count // 2)):
        if halves:
            pair_rows = pair(halves[0], rows, got)
            members = [pair_rows] + [places.along_y(pair_rows, d) for d in y_shifts[1:]]
        some = chunks[first : first + count // 2]
        skips = [ko.shape[0] * TB * (first + i in early) for i in range(len(some))]
        keys, kmarks = (ko, kx), (kmark_o, kmark_x)
        halves.append(forward(name, first, skips, some, keys, kmarks, qmark, cols, 3 * 10**9))
    stat = whole(y_shifts, members, halves[1])
    key_partner = backward("backward_partner", kx, chunks, kmark_x, qmark, stat)
    key_got = places.key_partner(key_partner)

    made = shares(count, len(far), early, key_partner, stat, rows, early_rows, *halves, early_out)
    sends, far_partners = made[:count], made[count:]
    row_parts = [sends[0]] + [places.along_y(part, -d) for part, d in zip(sends[1:], near)]
    far_parts = sends[len(row_parts) :]
    far_got = [places.query_partner(far_rows) for far_rows in far_partners]
    key_own = backward("backward_own", ko, chunks, kmark_o, qmark, stat)
    far_parts = [
        places.along_y(far_sum(part, got, key_own), -d)
        for part, got, d in zip(far_parts, far_got, far)
    ]

    key_parts = add(key_own, key_got, "add_keys", stat)
    key_parts = [key_parts[0]] + [
        places.along_z(part, -d) for part, d in zip(key_parts[1:], z_shifts[1:])
    ]
    row_got = places.query_partner(partner_sum(row_parts, key_own))
    attn, grad_queries = sum_parts(row_parts + far_parts + [row_got], "sum_rows")
    other_attn = lax.ppermute(attn, "head", swap)
    mixed_output, token = project(attn, other_attn, out_weight, other_weight)
    grad_keys, grad_values = sum_parts(key_parts, "sum_keys", (token,))
    return (mixed_output, grad_queries, grad_keys, grad_values)


def solution(mesh):
    tokens = P(("row", "col"))
    heads = P(("row", "col"), "head")
    whole = P(("row", "col"), None)
    places = Places(mesh.shape["row"], mesh.shape["col"])
    return jax.shard_map(
        functools.partial(on_device, places),
        mesh=mesh,
        in_specs=(heads, heads, heads, tokens, P("head", None), whole),
        out_specs=(whole, heads, heads, heads),
        check_vma=False,
    )
```

```python
import functools
import math

import jax
import jax.numpy as jnp
from jax import lax
from jax.experimental import pallas as pl
from jax.experimental.pallas import tpu as pltpu
from jax.sharding import PartitionSpec as P

HD = 128
TB = 128
HP = 3
PR = 2 * HP * TB
SR = 16
SCALE = 1.0 / math.sqrt(HD)
C2 = SCALE * math.log2(math.e)
FAR = 128.0
SEGS = 8
VMEM_BYTES = 12 * 1024 * 1024
ALL_VMEM = 63_000_000
F32 = jnp.float32
BF16 = jnp.bfloat16
WHOLE = pl.BlockSpec(memory_space=pltpu.VMEM)
ANYWHERE = pl.BlockSpec(memory_space=pl.ANY)


def call(
    kernel, name, out_shape, args, scratch=(), anywhere=0, vmem=VMEM_BYTES, flops=0, moved=0, exps=0
):
    return pl.pallas_call(
        kernel,
        out_shape=out_shape,
        in_specs=[ANYWHERE] * anywhere + [WHOLE] * (len(args) - anywhere),
        out_specs=jax.tree.map(lambda _: WHOLE, out_shape),
        scratch_shapes=list(scratch),
        compiler_params=pltpu.CompilerParams(vmem_limit_bytes=vmem),
        cost_estimate=pl.CostEstimate(flops=flops, bytes_accessed=moved, transcendentals=exps),
        name=name,
    )(*args)


def shape(dims, dtype):
    return jax.ShapeDtypeStruct(dims, dtype)


def dot_nn(a, b):
    return lax.dot_general(a, b, (((1,), (0,)), ((), ())), preferred_element_type=F32)


def dot_nt(a, b):
    return lax.dot_general(a, b, (((1,), (1,)), ((), ())), preferred_element_type=F32)


def write_block(first, second, seg_ref, out_ref):
    for h in range(HP):
        cols = slice(h * HD, (h + 1) * HD)
        out_ref[h * TB : (h + 1) * TB, :] = first[:, cols]
        out_ref[(HP + h) * TB : (HP + h + 1) * TB, :] = second[:, cols]
    out_ref[PR : PR + SR, :] = jnp.broadcast_to(seg_ref[...].astype(F32), (SR, TB)).astype(BF16)


def fetch(sources, held, sems):
    copies = [pltpu.make_async_copy(a, b, sems.at[i]) for i, (a, b) in enumerate(zip(sources, held))]
    for copy in copies:
        copy.start()
    for copy in copies:
        copy.wait()


def pack_kernel(*refs):
    sources, (kv_ref, qg_ref), (*held, sems) = refs[:6], refs[6:8], refs[8:]
    fetch(sources, held, sems)
    seg, key, value, query, grad, weight = held
    write_block(key[...], value[...], seg, kv_ref)
    write_block(query[...], dot_nt(grad[...], weight[...]).astype(BF16), seg, qg_ref)


def pack(*args):
    block = shape((PR + SR, HD), BF16)
    scratch = [pltpu.VMEM(a.shape, a.dtype) for a in args] + [pltpu.SemaphoreType.DMA((len(args),))]
    return call(pack_kernel, "pack", (block, block), args, scratch, len(args), ALL_VMEM)


def fill_marks(part_refs, mark_ref, for_keys):
    place = lax.broadcasted_iota(jnp.int32, (TB, TB), 0).astype(F32)
    start = 0
    for part_ref in part_refs:
        for b in range(part_ref.shape[0]):
            seg = part_ref[b, PR : PR + SR, :][0:1].astype(F32)
            if for_keys:
                marks = jnp.where((place != seg) & (place < SEGS), -FAR, 0.0)
            else:
                marks = jnp.where(place == seg, FAR, 0.0)
            mark_ref[start : start + TB, :] = jnp.transpose(marks).astype(BF16)
            start += TB


def head_rows(refs, slot):
    return jnp.concatenate(
        [
            ref[:, slot * TB : (slot + 1) * TB, :].reshape(ref.shape[0] * TB, HD)
            for ref in refs
        ],
        axis=0,
    )


STEP = 2
ROWS = STEP * TB


def merge(first, second):
    top = jnp.maximum(first[0], second[0])
    norm = top + jnp.log2(jnp.exp2(first[0] - top) + jnp.exp2(second[0] - top))
    delta = jnp.exp2(first[0] - norm) * first[1] + jnp.exp2(second[0] - norm) * second[1]
    return norm, delta


def chunk_rows(ref, slot):
    return ref[:, slot * TB : (slot + 1) * TB, :].reshape(ROWS, HD)


def stats_part(tasks, qmark, cols_ref, rows_ref):
    for h in range(HP):
        for key_refs, kmarks, chunks in tasks:
            marks = jnp.concatenate([m[...] for m in kmarks], axis=0)
            k = jnp.concatenate([head_rows(key_refs, h), marks], axis=1)
            v = head_rows(key_refs, HP + h)
            for chunk, i in chunks:
                here = slice(i * ROWS, (i + 1) * ROWS)
                q, g = chunk_rows(chunk, h), chunk_rows(chunk, HP + h)
                scores = dot_nt(jnp.concatenate([q, qmark[here, :]], axis=1), k)
                top = jnp.max(scores, axis=1, keepdims=True)
                e = jnp.exp2((scores - top) * C2)
                cols_ref[here, 3 * h : 3 * h + 1] = top
                cols_ref[here, 3 * h + 1 : 3 * h + 2] = jnp.sum(e, axis=1, keepdims=True)
                cols_ref[here, 3 * h + 2 : 3 * h + 3] = jnp.sum(
                    e * dot_nt(g, v), axis=1, keepdims=True
                )
    found = jnp.transpose(cols_ref[...])
    rows_ref[...] = jnp.zeros_like(rows_ref)
    for h in range(HP):
        top, total, delta = (found[r : r + 1, :] for r in range(3 * h, 3 * h + 3))
        rows_ref[2 * h : 2 * h + 1, :] = top * C2 + jnp.log2(total)
        rows_ref[2 * h + 1 : 2 * h + 2, :] = delta / total


def rows_to_cols(rows_ref, cols_ref):
    rows = rows_ref[...]
    rest = jnp.zeros((HD - rows.shape[0], rows.shape[1]), F32)
    cols_ref[...] = jnp.transpose(jnp.concatenate([rows, rest], axis=0))


def early_stats_kernel(*refs):
    *chunks, key_ref, cols_ref, rows_ref, qmark, kmark = refs
    fill_marks(chunks, qmark, False)
    fill_marks((key_ref,), kmark, True)
    chunks = [(chunk, i) for i, chunk in enumerate(chunks)]
    stats_part([((key_ref,), (kmark,), chunks)], qmark, cols_ref, rows_ref)
    rows_to_cols(rows_ref, cols_ref)


def all_stats_kernel(early, count, *refs):
    chunks, refs = refs[:count], refs[count:]
    ko_ref, kx_ref, kmark_o, early_mark, before_ref, cols_ref, rows_ref, qmark, kmark_x = refs
    fill_marks((kx_ref,), kmark_x, True)
    late = [i for i in range(count) if i not in early]
    for j, i in enumerate(early):
        qmark[i * ROWS : (i + 1) * ROWS, :] = early_mark[j * ROWS : (j + 1) * ROWS, :]
    for i in late:
        fill_marks((chunks[i],), qmark.at[i * ROWS : (i + 1) * ROWS, :], False)
    tasks = [
        ((kx_ref,), (kmark_x,), [(chunks[i], i) for i in early]),
        ((ko_ref, kx_ref), (kmark_o, kmark_x), [(chunks[i], i) for i in late]),
    ]
    stats_part(tasks, qmark, cols_ref, rows_ref)
    for j, i in enumerate(early):
        then, here = slice(j * ROWS, (j + 1) * ROWS), slice(i * ROWS, (i + 1) * ROWS)
        for r in range(0, 2 * HP, 2):
            norm, delta = merge(
                (before_ref[r : r + 1, then], before_ref[r + 1 : r + 2, then]),
                (rows_ref[r : r + 1, here], rows_ref[r + 1 : r + 2, here]),
            )
            rows_ref[r : r + 1, here] = norm
            rows_ref[r + 1 : r + 2, here] = delta
    rows_to_cols(rows_ref, cols_ref)


def early_stats(chunks, key):
    n, m = len(chunks) * ROWS, key.shape[0] * TB
    out = (shape((n, HD), F32), shape((8, n), F32), shape((n, HD), BF16), shape((m, HD), BF16))
    return call(early_stats_kernel, "stats_early", out, (*chunks, key))


def all_stats(early, chunks, *args):
    n, m = len(chunks) * ROWS, args[1].shape[0] * TB
    out = (shape((n, HD), F32), shape((8, n), F32), shape((n, HD), BF16), shape((m, HD), BF16))
    kernel = functools.partial(all_stats_kernel, early, len(chunks))
    return call(kernel, "stats_all", out, (*chunks, *args))


def forward_kernel(first, skips, parts, *refs):
    count = len(skips)
    chunks, keys, refs = refs[:count], refs[count : count + parts], refs[count + parts :]
    kmarks, (qmark, norm_ref, out_ref) = refs[:parts], refs[parts:]
    marks = jnp.concatenate([m[...] for m in kmarks], axis=0)
    for h in range(HP):
        k = head_rows(keys, h)
        v = head_rows(keys, HP + h)
        k_marked = jnp.concatenate([k, marks], axis=1)
        vk = jnp.concatenate([v, k], axis=1)
        for i, (chunk, skip) in enumerate(zip(chunks, skips)):
            here = slice(i * ROWS, (i + 1) * ROWS)
            there = slice((first + i) * ROWS, (first + i + 1) * ROWS)
            q, g = chunk_rows(chunk, h), chunk_rows(chunk, HP + h)
            scores = dot_nt(jnp.concatenate([q, qmark[there, :]], axis=1), k_marked[skip:])
            p = jnp.exp2(scores * C2 - norm_ref[there, 2 * h : 2 * h + 1])
            mix = p * dot_nt(g, v[skip:])
            out_ref[h, here, : 2 * HD] = dot_nn(p.astype(BF16), vk[skip:])
            out_ref[h, here, 2 * HD :] = dot_nn(mix.astype(BF16), k[skip:])


def forward(name, first, skips, chunks, keys, kmarks, qmark, cols, flops=0):
    n = len(chunks) * ROWS
    return call(
        functools.partial(forward_kernel, first, skips, len(keys)), name,
        shape((HP, n, 3 * HD), F32), (*chunks, *keys, *kmarks, qmark, cols), flops=flops,
    )


def pair_kernel(later_ref, *refs):
    del later_ref
    mine_ref, got_ref, out_ref = refs
    out_ref[...] = jnp.zeros_like(out_ref)
    for block in range(mine_ref.shape[1] // TB):
        mine = slice(block * TB, (block + 1) * TB)
        theirs = slice((block ^ 1) * TB, ((block ^ 1) + 1) * TB)
        for r in range(0, 2 * HP, 2):
            norm, delta = merge(
                (mine_ref[r : r + 1, mine], mine_ref[r + 1 : r + 2, mine]),
                (got_ref[r : r + 1, theirs], got_ref[r + 1 : r + 2, theirs]),
            )
            out_ref[r : r + 1, mine] = norm
            out_ref[r + 1 : r + 2, mine] = delta


def pair(later, mine, got):
    return call(pair_kernel, "pair_rows", shape(mine.shape, F32), (later, mine, got), anywhere=1)


def whole_kernel(steps, later_ref, *refs):
    del later_ref
    *members, stat_ref = refs
    stat_ref[...] = jnp.zeros_like(stat_ref)
    for i, mine in enumerate(steps):
        here = slice(i * ROWS, (i + 1) * ROWS)
        found = []
        for member, step in zip(members, steps):
            at = steps.index((mine - step) % len(steps)) * ROWS
            found.append(member[:, at : at + ROWS])
        for r in range(0, 2 * HP, 2):
            norm, delta = functools.reduce(merge, [(f[r : r + 1], f[r + 1 : r + 2]) for f in found])
            stat_ref[r : r + 1, here] = norm
            stat_ref[r + 1 : r + 2, here] = delta


def whole(steps, members, later):
    out = shape(members[0].shape, F32)
    return call(functools.partial(whole_kernel, steps), "whole_rows", out, (later, *members), anywhere=1)


def share_kernel(chunks, early, later_ref, stat_ref, rows_ref, early_rows, *refs):
    del later_ref
    outs, early_out, sends, partners = refs[:2], refs[2], refs[3 : 3 + chunks], refs[3 + chunks :]
    partners = [None] * (chunks - len(partners)) + list(partners)
    rows = []
    for r in range(0, 2 * HP, 2):
        rows.append(jnp.exp2(rows_ref[r : r + 1, :] - stat_ref[r : r + 1, :]))
        rows.append(stat_ref[r + 1 : r + 2, :])
        parts = [jnp.zeros((1, ROWS), F32)] * chunks
        for j, i in enumerate(early):
            then, here = slice(j * ROWS, (j + 1) * ROWS), slice(i * ROWS, (i + 1) * ROWS)
            parts[i] = jnp.exp2(early_rows[r : r + 1, then] - stat_ref[r : r + 1, here])
        rows.append(jnp.concatenate(parts, axis=1))
    rows.append(jnp.zeros((TB - 3 * HP, chunks * ROWS), F32))
    cols = jnp.transpose(jnp.concatenate(rows, axis=0))
    for i, send_ref in enumerate(sends):
        here = slice(i * ROWS, (i + 1) * ROWS)
        out_ref, start = outs[i // (chunks // 2)], i % (chunks // 2) * ROWS
        there = slice(start, start + ROWS)
        for h in range(HP):
            share, delta, early_share = (cols[here, 3 * h + c : 3 * h + c + 1] for c in range(3))
            attn, plain, mixed = (
                share * out_ref[h, there, c * HD : (c + 1) * HD] for c in range(3)
            )
            if i in early:
                then = slice(early.index(i) * ROWS, (early.index(i) + 1) * ROWS)
                more = [
                    early_share * early_out[h, then, c * HD : (c + 1) * HD] for c in range(3)
                ]
                attn, plain, mixed = attn + more[0], plain + more[1], mixed + more[2]
            attn = attn.astype(BF16)
            grad = (SCALE * (mixed - delta * plain)).astype(BF16)
            for slot, value in ((h, attn), (HP + h, grad)):
                there_rows = slice(slot * TB, (slot + 1) * TB)
                send_ref[0, there_rows, :] = value[:TB]
                if partners[i] is None:
                    send_ref[1, there_rows, :] = value[TB:]
                else:
                    partners[i][there_rows, :] = value[TB:]


def shares(chunks, far, early, later, *args):
    out = (shape((STEP, PR, HD), BF16),) * (chunks - far) + (shape((1, PR, HD), BF16),) * far
    out += (shape((PR, HD), BF16),) * far
    return call(
        functools.partial(share_kernel, chunks, early), "share_rows", out, (later, *args),
        anywhere=1, moved=4 * 2**20,
    )


def backward_kernel(count, k_ref, *refs):
    chunks, (kmark, qmark, stat_ref, send_ref) = refs[:count], refs[count:]
    marks = qmark[...]
    for h in range(HP):
        q = head_rows(chunks, h)
        g = head_rows(chunks, HP + h)
        q_marked = jnp.concatenate([q, marks], axis=1)
        norm, delta = (stat_ref[r : r + 1, :] for r in (2 * h, 2 * h + 1))

        for i in range(k_ref.shape[0] // STEP):
            here = slice(i * ROWS, (i + 1) * ROWS)
            these = slice(i * STEP, (i + 1) * STEP)
            k, v = (
                k_ref[these, slot * TB : (slot + 1) * TB, :].reshape(ROWS, HD)
                for slot in (h, HP + h)
            )
            scores = dot_nt(jnp.concatenate([k, kmark[here, :]], axis=1), q_marked)
            probs = jnp.exp2(scores * C2 - norm)
            change = probs * (dot_nt(v, g) - delta)
            grad_k = (dot_nn(change.astype(BF16), q) * SCALE).astype(BF16)
            grad_v = dot_nn(probs.astype(BF16), g).astype(BF16)
            send_ref[these, h * TB : (h + 1) * TB, :] = grad_k.reshape(STEP, TB, HD)
            send_ref[these, (HP + h) * TB : (HP + h + 1) * TB, :] = grad_v.reshape(STEP, TB, HD)


def backward(name, k, chunks, kmark, qmark, stat):
    n, m = len(chunks) * ROWS, k.shape[0] * TB
    args = (k, *chunks, kmark, qmark, stat)
    return call(
        functools.partial(backward_kernel, len(chunks)), name,
        shape((k.shape[0], PR, HD), BF16), args,
        flops=10 * n * m * 2 * HD * HP, moved=8 * 2**20, exps=n * m * HP,
    )


def partner_sum_kernel(later_ref, *refs):
    del later_ref
    refs[-1][...] = sum(ref[1].astype(F32) for ref in refs[:-1]).astype(BF16)


def partner_sum(parts, later):
    return call(
        partner_sum_kernel, "sum_partner", shape((PR, HD), BF16), (later, *parts), anywhere=1,
        moved=len(parts) * PR * HD * 2,
    )


def far_sum_kernel(later_ref, mine_ref, got_ref, out_ref):
    del later_ref
    out_ref[...] = (mine_ref[0].astype(F32) + got_ref[...].astype(F32)).astype(BF16)


def far_sum(mine, got, later):
    args = (later, mine, got)
    return call(far_sum_kernel, "sum_far", shape((PR, HD), BF16), args, anywhere=1)


def add_kernel(later_ref, own_ref, got_ref, *out_refs):
    del later_ref
    for j, out_ref in enumerate(out_refs):
        out_ref[...] = (own_ref[j].astype(F32) + got_ref[j].astype(F32)).astype(BF16)


def add(own, got, name, later):
    out = tuple(shape(own.shape[1:], BF16) for _ in range(own.shape[0]))
    args = (later, own, got)
    return call(add_kernel, name, out, args, anywhere=1, flops=own.size, moved=6 * own.size)


def sum_kernel(skip, *refs):
    parts, (first_ref, second_ref) = refs[skip:-2], refs[-2:]
    parts = [part[0] if len(part.shape) == 3 else part[...] for part in parts]
    total = sum(part.astype(F32) for part in parts).astype(BF16)
    for h in range(HP):
        cols = slice(h * HD, (h + 1) * HD)
        first_ref[:, cols] = total[h * TB : (h + 1) * TB, :]
        second_ref[:, cols] = total[(HP + h) * TB : (HP + h + 1) * TB, :]


def sum_parts(parts, name, later=()):
    out = shape((TB, HP * HD), BF16)
    size = sum(p.size for p in parts)
    kernel, args = functools.partial(sum_kernel, len(later)), (*later, *parts)
    return call(kernel, name, (out, out), args, anywhere=len(later), flops=size, moved=2 * size)


def project_kernel(own_ref, other_ref, own_weight, other_weight, out_ref, token_ref):
    token_ref[...] = jnp.zeros_like(token_ref)
    out_ref[...] = (
        dot_nn(own_ref[...], own_weight[...]) + dot_nn(other_ref[...], other_weight[...])
    ).astype(BF16)


def project(own, other, own_weight, other_weight):
    width = own_weight.shape[1]
    return call(
        project_kernel, "project", (shape((TB, width), BF16), shape((8, HD), F32)),
        (own, other, own_weight, other_weight),
        flops=4 * own.size * width, moved=4 * own_weight.size,
    )


class Places:
    def __init__(self, n_row, n_col):
        self.n_row, self.n_col = n_row, n_col
        self.ny, self.nz = n_col // 2, n_row // 2

    def of(self, index):
        row, col = divmod(index, self.n_col)
        low, z = divmod(row, self.nz)
        y, high = divmod(col, 2)
        return high, low, y, z

    def index(self, high, low, y, z):
        return (low * self.nz + z) * self.n_col + y * 2 + high

    def send(self, array, move):
        pairs = []
        for i in range(self.n_row * self.n_col):
            for core in range(2):
                target = self.index(*move(core, *self.of(i)))
                pairs.append((2 * i + core, 2 * target + core))
        return lax.ppermute(array, ("row", "col", "head"), pairs)

    def along_y(self, array, by):
        return self.send(array, lambda core, high, low, y, z: (high, low, (y + by) % self.ny, z))

    def along_z(self, array, by):
        return self.send(array, lambda core, high, low, y, z: (high, low, y, (z + by) % self.nz))

    def query_partner(self, array):
        return self.send(array, lambda core, high, low, y, z: (high ^ 1 ^ core, low ^ 1, y, z))

    def query_partner_along_y(self, array, by):
        return self.send(
            array,
            lambda core, high, low, y, z: (high ^ 1 ^ core, low ^ 1, (y + by) % self.ny, z),
        )

    def key_partner(self, array):
        return self.send(array, lambda core, high, low, y, z: (high ^ core, low ^ 1, y, z))


def shifts(n):
    return [0] + sorted(range(1, n), key=lambda d: min(d, n - d))


def on_device(places, query, key, value, segment_ids, out_weight, grad_output):
    swap = [(0, 1), (1, 0)]
    y_shifts, z_shifts = shifts(places.ny), shifts(places.nz)
    seg = segment_ids.reshape(1, TB)

    kv, qg = pack(seg, key, value, query, grad_output, out_weight)
    pair0 = jnp.stack([qg, places.query_partner(qg)])
    far = [d for d in y_shifts if 1 < d == places.ny - d]
    near = [d for d in y_shifts[1:] if d not in far]
    chunks = [pair0] + [places.along_y(pair0, d) for d in near]
    far_blocks = [places.along_y(qg, d) for d in far]
    far_partner_blocks = [places.query_partner_along_y(qg, d) for d in far]
    chunks += [jnp.stack(pair) for pair in zip(far_blocks, far_partner_blocks)]
    key_blocks = [places.along_z(kv, d) for d in z_shifts[1:]]
    (kv, *key_blocks), *_ = lax.optimization_barrier(
        ((kv, *key_blocks), pair0, *far_blocks, *far_partner_blocks)
    )
    ko = jnp.stack([kv] + key_blocks)
    kx = places.key_partner(ko)
    other_weight = lax.ppermute(out_weight, "head", swap)

    count = len(chunks)
    early = [i for i in range(count) if not 1 <= i <= len(near)]
    some = [chunks[i] for i in early]
    early_cols, early_rows, early_mark, kmark_o = early_stats(some, ko)
    early_out = forward(
        "forward_early", 0, [0] * len(early), some, [ko], [kmark_o], early_mark, early_cols
    )
    early_rows, _ = lax.optimization_barrier((early_rows, early_out))
    cols, rows, qmark, kmark_x = all_stats(early, chunks, ko, kx, kmark_o, early_mark, early_rows)
    got = places.query_partner(rows)
    halves = []
    for name, first in (("forward_near", 0), ("forward_far", count // 2)):
        if halves:
            pair_rows = pair(halves[0], rows, got)
            members = [pair_rows] + [places.along_y(pair_rows, d) for d in y_shifts[1:]]
        some = chunks[first : first + count // 2]
        skips = [ko.shape[0] * TB * (first + i in early) for i in range(len(some))]
        keys, kmarks = (ko, kx), (kmark_o, kmark_x)
        halves.append(forward(name, first, skips, some, keys, kmarks, qmark, cols, 3 * 10**9))
    stat = whole(y_shifts, members, halves[1])
    key_partner = backward("backward_partner", kx, chunks, kmark_x, qmark, stat)
    key_got = places.key_partner(key_partner)

    made = shares(count, len(far), early, key_partner, stat, rows, early_rows, *halves, early_out)
    sends, far_partners = made[:count], made[count:]
    row_parts = [sends[0]] + [places.along_y(part, -d) for part, d in zip(sends[1:], near)]
    far_parts = sends[len(row_parts) :]
    far_got = [places.query_partner(far_rows) for far_rows in far_partners]
    key_own = backward("backward_own", ko, chunks, kmark_o, qmark, stat)
    far_parts = [
        places.along_y(far_sum(part, got, key_own), -d)
        for part, got, d in zip(far_parts, far_got, far)
    ]

    key_parts = add(key_own, key_got, "add_keys", stat)
    key_parts = [key_parts[0]] + [
        places.along_z(part, -d) for part, d in zip(key_parts[1:], z_shifts[1:])
    ]
    row_got = places.query_partner(partner_sum(row_parts, key_own))
    attn, grad_queries = sum_parts(row_parts + far_parts + [row_got], "sum_rows")
    other_attn = lax.ppermute(attn, "head", swap)
    mixed_output, token = project(attn, other_attn, out_weight, other_weight)
    grad_keys, grad_values = sum_parts(key_parts, "sum_keys", (token,))
    return (mixed_output, grad_queries, grad_keys, grad_values)


def solution(mesh):
    tokens = P(("row", "col"))
    heads = P(("row", "col"), "head")
    whole = P(("row", "col"), None)
    places = Places(mesh.shape["row"], mesh.shape["col"])
    return jax.shard_map(
        functools.partial(on_device, places),
        mesh=mesh,
        in_specs=(heads, heads, heads, tokens, P("head", None), whole),
        out_specs=(whole, heads, heads, heads),
        check_vma=False,
    )
```
